32 devices in a mesh: gx: 4 (over y, core), gy: 4 (over z), gz: 2 (over x).
Axes of the slice: x: 2, y: 2, z: 4, core: 2. Of those that a mesh axis runs over, the one named last changes fastest.
Arguments:
- mode_shapes: bfloat16 [3, 16, 16, 32, 256], P(None, None, 'gx', 'gy', 'gz'), may hold values from -4 to 4
- stress_field: float32 [6, 16, 32, 256], P(None, 'gx', 'gy', 'gz'), may hold values from -6 to 6
- displacement: float32 [3, 16, 32, 256], P(None, 'gx', 'gy', 'gz'), may hold values from -6 to 6
- material: int32 [16, 32, 256], P('gx', 'gy', 'gz'), may hold values from 0 to 7
- fixed_nodes: int32 [16, 32, 256], P('gx', 'gy', 'gz'), may hold values 0 or 1
- eigenvalues: float32 [16], replicated, may hold values from 0.5 to 4
- mode_weight: float32 [16], replicated, may hold values from 0.2 to 1
Outputs:
- mode_sens: float32 [16, 16, 32, 256], P(None, 'gx', 'gy', 'gz')
- adjoint_term: float32 [16, 32, 256], P('gx', 'gy', 'gz')
The draws below stay inside these ranges and needn't reach their ends.
All inputs are finite; a program needn't handle non-finite values. No bound on the sum of `fixed_nodes` on one device may be relied on, other than what follows from the above.
Results may differ from the reference program's by a relative error of at most 0.00035.
Values may be sent and summed in bfloat16 or wider, within the bound.
No kernel may reach another device: no remote copies, remote signals or barrier semaphores. Data moves between devices by JAX's collectives and lax.ppermute only.
A program may use at most 64 MiB of HBM per device.

```python
import math
import jax
import jax.numpy as jnp
import numpy as np
from jax import lax

MODES = 16
LEVELS = 8
NX = 16
NY = 32
NZ = 256


def place_ends(entries, own_key, low, largest):
    dims = entries.shape
    index_at = [jax.random.randint(jax.random.fold_in(own_key, axis), (), 0, dims[axis]) for axis in range(len(dims))]
    entries = entries.at[tuple(index_at)].set(low)
    longest = dims.index(max(dims))
    index_at[longest] = (index_at[longest] + 1) % dims[longest]
    return entries.at[tuple(index_at)].set(largest)


def block_levels(rng, dims, shards, smallest, top_value):
    level = 1.0
    for position, parts in shards:
        draws = jax.random.uniform(jax.random.fold_in(jax.random.fold_in(rng, 6), position), (parts,), jnp.float32, smallest / len(shards), top_value / len(shards))
        level = level * jnp.repeat(jnp.exp(draws), dims[position] // parts).reshape((-1,) + (1,) * (len(dims) - 1 - position))
    return level


def bell_draw(rng, dims, deviation, limit, cuts=(), kind=jnp.bfloat16):
    entries = deviation * jax.random.normal(rng, dims, jnp.float32)
    if cuts:
        entries = entries * block_levels(rng, dims, cuts, -0.22, 0.18)
    return jnp.clip(entries, -limit, limit).astype(kind)


def setup_inputs(seed: int = 0) -> dict:
    key_list = jax.random.split(jax.random.key(seed), 8)
    mode_shapes = bell_draw(key_list[0], (3, MODES, NX, NY, NZ), 0.3, 4.0, ((2, 4), (3, 4), (4, 2)))
    stress_field = bell_draw(key_list[1], (6, NX, NY, NZ), 1.0, 6.0, ((1, 4), (2, 4), (3, 2)), jnp.float32)
    displacement = bell_draw(key_list[2], (3, NX, NY, NZ), 1.0, 6.0, ((1, 4), (2, 4), (3, 2)), jnp.float32)
    material = place_ends(jax.random.randint(key_list[3], (NX, NY, NZ), 0, LEVELS), jax.random.fold_in(key_list[3], 1), 0, LEVELS - 1).astype(jnp.int32)
    fixed_nodes = place_ends((jax.random.randint(key_list[4], (NX, NY, NZ), 0, 8) < 1).astype(jnp.int32), jax.random.fold_in(key_list[4], 1), 0, 1)
    eigenvalues = jnp.clip(jnp.exp(jax.random.uniform(key_list[5], (MODES,), jnp.float32, math.log(0.5), math.log(4.0))), 0.5, 4.0)
    mode_weight = jnp.clip(jnp.exp(jax.random.uniform(key_list[6], (MODES,), jnp.float32, math.log(0.2), math.log(1.0))), 0.2, 1.0)
    return {"mode_shapes": mode_shapes, "stress_field": stress_field, "displacement": displacement, "material": material, "fixed_nodes": fixed_nodes, "eigenvalues": eigenvalues, "mode_weight": mode_weight}


corner_list = [(a, b, c) for a in (0, 1) for b in (0, 1) for c in (0, 1)]

def shape_value(side, point):
    return point if side else 1.0 - point

def shape_slope(side):
    return 1.0 if side else -1.0

def strain_matrix(point_x, point_y, point_z):
    deriv = np.zeros((3, 8))
    for node, (a, b, c) in enumerate(corner_list):
        value_x = shape_value(a, point_x)
        value_y = shape_value(b, point_y)
        value_z = shape_value(c, point_z)
        deriv[0, node] = shape_slope(a) * value_y * value_z
        deriv[1, node] = value_x * shape_slope(b) * value_z
        deriv[2, node] = value_x * value_y * shape_slope(c)
    matrix = np.zeros((6, 24))
    for node in range(8):
        column = 3 * node
        matrix[0, column] = deriv[0, node]
        matrix[1, column + 1] = deriv[1, node]
        matrix[2, column + 2] = deriv[2, node]
        matrix[3, column + 1] = deriv[2, node]
        matrix[3, column + 2] = deriv[1, node]
        matrix[4, column] = deriv[2, node]
        matrix[4, column + 2] = deriv[0, node]
        matrix[5, column] = deriv[1, node]
        matrix[5, column + 1] = deriv[0, node]
    return (matrix, deriv)

def tables():
    poisson = 0.45
    lame_first = poisson / ((1.0 + poisson) * (1.0 - 2.0 * poisson))
    lame_second = 0.5 / (1.0 + poisson)
    elastic = np.zeros((6, 6))
    elastic[:3, :3] = lame_first
    for axis_k in range(3):
        elastic[axis_k, axis_k] += 2.0 * lame_second
        elastic[axis_k + 3, axis_k + 3] = lame_second
    offset = 0.5 / math.sqrt(3.0)
    points = [0.5 - offset, 0.5 + offset]
    pairs = [(0, 0), (1, 1), (2, 2), (1, 2), (0, 2), (0, 1)]
    stiffness = np.zeros((24, 24))
    geometric = np.zeros((6, 24, 24))
    for point_x in points:
        for point_y in points:
            for point_z in points:
                matrix, deriv = strain_matrix(point_x, point_y, point_z)
                stiffness += 0.125 * matrix.T @ elastic @ matrix
                for comp, (first, second) in enumerate(pairs):
                    outer = np.outer(deriv[first], deriv[second])
                    if first != second:
                        outer = outer + outer.T
                    geometric[comp] += 0.125 * np.kron(outer, np.eye(3))
    center, unused = strain_matrix(0.5, 0.5, 0.5)
    coupling = elastic @ center
    return (jnp.asarray(stiffness, jnp.float32), jnp.asarray(geometric, jnp.float32), jnp.asarray(coupling, jnp.float32))

def element_block(node_slab, cell_data, eigenvalues, mode_weight, k_base, g_base, coupling):
    highest = lax.Precision.HIGHEST
    mode_count = node_slab.shape[1]
    count_y = cell_data.shape[1]
    count_z = cell_data.shape[2]
    total = count_y * count_z
    width = -(-total // 128) * 128
    extra = width - total
    pieces = [node_slab[:, :, a, b:b + count_y, c:c + count_z] for a, b, c in corner_list]
    dofs = jnp.stack(pieces, 0).reshape(24, mode_count, total)
    dofs = jnp.pad(dofs, ((0, 0), (0, 0), (0, extra)))
    big_table = jnp.concatenate([k_base[None], g_base], 0).reshape(168, 24)
    products = jnp.einsum('rs,sme->rme', big_table, dofs, precision=highest).reshape(7, 24, mode_count, width)
    forms = lax.optimization_barrier(jnp.sum(products * dofs[None], 1))
    energy = forms[0]
    quad = forms[1:]
    flat_cells = jnp.pad(cell_data.reshape(9, total), ((0, 0), (0, extra)))
    projected = jnp.einsum('ce,cme->me', flat_cells[:6], quad, precision=highest)
    sensitivity = flat_cells[7] * energy - eigenvalues[:, None] * flat_cells[8] * projected
    coefficient = jnp.einsum('m,cme->ce', mode_weight * eigenvalues, quad, precision=highest)
    forces = -flat_cells[6] * jnp.dot(coupling.T, coefficient, precision=highest)
    return (sensitivity[:, :total].reshape(mode_count, count_y, count_z), forces[:, :total].reshape(24, count_y, count_z))

def element_term(node_slab, slope_layer, k_base):
    count_y = slope_layer.shape[0]
    count_z = slope_layer.shape[1]
    pieces = jnp.stack([node_slab[:, a, b:b + count_y, c:c + count_z] for a, b, c in corner_list], 0)
    load_dofs = pieces[:, :3].reshape(24, count_y * count_z)
    disp_dofs = pieces[:, 3:].reshape(24, count_y * count_z)
    product = jnp.dot(k_base, disp_dofs, precision=lax.Precision.HIGHEST)
    return slope_layer * lax.optimization_barrier(jnp.sum(load_dofs * product, 0)).reshape(count_y, count_z)

def assemble(forces):
    assembled = None
    for corner, (a, b, c) in enumerate(corner_list):
        portion = jnp.transpose(forces[:, 3 * corner:3 * corner + 3], (1, 0, 2, 3))
        portion = jnp.pad(portion, ((0, 0), (a, 1 - a), (b, 1 - b), (c, 1 - c)))
        assembled = portion if assembled is None else assembled + portion
    return assembled

def material_data(stress_field, material):
    density = (material.astype(jnp.float32) + 1.0) / LEVELS
    young_mod = 0.001 + density ** 3
    slope_mod = 3.0 * density ** 2
    ratio_mod = slope_mod / young_mod
    return jnp.concatenate([stress_field, young_mod[None], slope_mod[None], ratio_mod[None]], 0)

def reference(mode_shapes, stress_field, displacement, material, fixed_nodes, eigenvalues, mode_weight):
    k_base, g_base, coupling = tables()
    cell_data = material_data(stress_field, material)
    padded = jnp.pad(mode_shapes, ((0, 0), (0, 0), (0, 1), (0, 1), (0, 1)))

    def layer_at(index):
        node_slab = lax.dynamic_slice_in_dim(padded, index, 2, 2).astype(jnp.float32)
        cells_now = lax.dynamic_index_in_dim(cell_data, index, 1, keepdims=False)
        return element_block(node_slab, cells_now, eigenvalues, mode_weight, k_base, g_base, coupling)
    sensitivity, forces = lax.map(layer_at, jnp.arange(NX))
    mode_sens = jnp.transpose(sensitivity, (1, 0, 2, 3))
    load = assemble(forces)[:, :NX, :NY, :NZ] * (1.0 - fixed_nodes.astype(jnp.float32))
    stacked = jnp.pad(jnp.concatenate([load, displacement], 0), ((0, 0), (0, 1), (0, 1), (0, 1)))

    def term_at(index):
        node_slab = lax.dynamic_slice_in_dim(stacked, index, 2, 1)
        slope_layer = lax.dynamic_index_in_dim(cell_data[7], index, 0, keepdims=False)
        return element_term(node_slab, slope_layer, k_base)
    adjoint_term = lax.map(term_at, jnp.arange(NX))
    return (mode_sens, adjoint_term)
```

```python
import functools
import math

import jax
import jax.numpy as jnp
from jax import lax
from jax.experimental import pallas as pl
from jax.experimental.pallas import tpu as pltpu
from jax.sharding import PartitionSpec as P

LEVELS = 8
POISSON = 0.45
LAM = POISSON / ((1.0 + POISSON) * (1.0 - 2.0 * POISSON))
MU = 0.5 / (1.0 + POISSON)
R3 = 1.0 / math.sqrt(3.0)
F32 = jnp.float32
BF16 = jnp.bfloat16
MODES = 16
GROUPS = 4
LANES = 128


def lane_iota(shape=(MODES, LANES)):
    return lax.broadcasted_iota(jnp.int32, shape, len(shape) - 1)


def row_iota(shape):
    return lax.broadcasted_iota(jnp.int32, shape, 0)


def roll(value, shift, axis=1):
    size = value.shape[axis]
    if isinstance(shift, int):
        shift = shift % size
        if shift == 0:
            return value
    return pltpu.roll(value, shift, axis)


def place(axis):
    me = lax.axis_index(axis)
    size = lax.axis_size(axis)
    even = lax.rem(me, 2) == 0
    return even, me > 0, me < size - 1


def pack_kernel(dims, modes, material, fixed, disp, tiles, x1, x2, edge, ex1, ex2, raw):
    nx, ny = dims
    span = MODES * nx * ny
    part = nx * ny
    for c in range(3):
        raw[c * span : (c + 1) * span, :] = modes[c].astype(F32).reshape(span, LANES)
    base = 3 * span

    def channel(index, value):
        raw[base + index * part : base + (index + 1) * part, :] = value.reshape(part, LANES)

    channel(0, material[...].astype(F32) + 1.0)
    channel(1, 1.0 - fixed[...].astype(F32))
    for c in range(3):
        value = disp[c]
        head = value.astype(BF16).astype(F32)
        channel(2 + c, head)
        channel(5 + c, value - head)
    raw[base + 8 * part : base + 16 * part, :] = jnp.zeros((8 * part, LANES), F32)
    lane = lane_iota()

    @pl.loop(0, GROUPS * nx)
    def _(step):
        c = step // nx
        x = lax.rem(step, nx)
        row = c * span + x * ny
        ends = jnp.zeros((MODES, LANES), F32)
        for y in range(ny):
            value = raw[pl.ds(row + y, MODES, stride=part), :]
            tiles[c, x, y] = value.astype(BF16)
            ends = jnp.where((lane >= 3 * y) & (lane < 3 * y + 3), roll(value, 3 * y + 1), ends)
        edge[c, x] = ends.astype(BF16)

    even, _, _ = place("gx")
    for out, out_edge, upward in ((x1, ex1, even), (x2, ex2, jnp.logical_not(even))):
        for s in range(2):
            layer = jnp.where(upward, nx - 1, s)
            for c in range(GROUPS):
                out[c, s] = tiles[c, layer]
                out_edge[c, s] = edge[c, layer]


def pick(parity, lower, upper, first, second, use_lower, use_upper, none_lower, none_upper):
    odd = jnp.logical_not(parity)
    pl.when(jnp.logical_and(lower, parity))(lambda: use_lower(second))
    pl.when(jnp.logical_and(lower, odd))(lambda: use_lower(first))
    pl.when(jnp.logical_and(upper, parity))(lambda: use_upper(first))
    pl.when(jnp.logical_and(upper, odd))(lambda: use_upper(second))
    pl.when(jnp.logical_not(lower))(none_lower)
    pl.when(jnp.logical_not(upper))(none_upper)


def merge_kernel(dims, zcount, *refs):
    nx, ny = dims
    tiles, r1, r2 = refs[:3]
    rz = refs[3 : 3 + zcount]
    rz1 = refs[3 + zcount : 3 + 2 * zcount]
    rz2 = refs[3 + 2 * zcount : 3 + 3 * zcount]
    full, rim, y1, y2 = refs[3 + 3 * zcount :]
    xe, xlo, xup = place("gx")
    ze, zlo, zup = place("gz")
    ye, _, _ = place("gy")
    full[:, 1 : nx + 1] = tiles[...]

    def lower(ref):
        full[:, 0:1] = ref[:, 0:1]

    def upper(ref):
        full[:, nx + 1 : nx + 3] = ref[...]

    def no_lower():
        full[:, 0:1] = jnp.zeros_like(full[:, 0:1])

    def no_upper():
        full[:, nx + 1 : nx + 3] = jnp.zeros_like(full[:, nx + 1 : nx + 3])

    pick(xe, xlo, xup, r1, r2, lower, upper, no_lower, no_upper)

    lane = lane_iota()
    phase = lax.rem(lane, 3)
    even_f = ze.astype(F32)
    lo_f = zlo.astype(F32)
    up_f = zup.astype(F32)

    def merged(blocks):
        if len(blocks) == 1:
            first = blocks[0].astype(F32)
            return first * jnp.where(phase == 0, lo_f, up_f)
        first, second = (b.astype(F32) for b in blocks)
        low = (second * even_f + first * (1.0 - even_f)) * lo_f
        high = (first * even_f + second * (1.0 - even_f)) * up_f
        return jnp.where(phase == 0, low, high)

    for c in range(GROUPS):
        for x in range(nx):
            rim[c, x + 1] = merged([r[c, x] for r in rz])

        def rim_lower(refs, c=c):
            rim[c, 0] = merged([r[c, 0] for r in refs])

        def rim_upper(refs, c=c):
            for s in range(2):
                rim[c, nx + 1 + s] = merged([r[c, s] for r in refs])

        def rim_no_lower(c=c):
            rim[c, 0] = jnp.zeros((MODES, LANES), F32)

        def rim_no_upper(c=c):
            for s in range(2):
                rim[c, nx + 1 + s] = jnp.zeros((MODES, LANES), F32)

        pick(xe, xlo, xup, rz1, rz2, rim_lower, rim_upper, rim_no_lower, rim_no_upper)

    width = nx + 3
    for out, upward in ((y1, ye), (y2, jnp.logical_not(ye))):
        rows = [jnp.where(upward, ny - 1, s) for s in range(2)]
        for c in range(GROUPS):
            ends = jnp.zeros((MODES, LANES), F32)
            for x in range(width):
                for s in range(2):
                    out[(c * width + x) * 2 + s] = full[c, x, rows[s]]
                    start = 16 * x + 3 * s
                    turned = roll(rim[c, x], lax.rem(start + LANES - 3 * rows[s], LANES))
                    ends = jnp.where((lane >= start) & (lane < start + 3), turned, ends)
            out[GROUPS * width * 2 + c] = ends.astype(BF16)


def cross_xy(a, b):
    return a[0] * b[1] + a[4] * b[5]


def cross_xz(a, b):
    return a[0] * b[2] + a[3] * b[5]


def cross_yz(a, b):
    return a[1] * b[2] + a[3] * b[4]


def squares(a):
    f, g, h, t = a[3] * a[3], a[4] * a[4], a[5] * a[5], a[6] * a[6]
    ft = f + t
    return (a[0] * a[0] + (ft + g), a[1] * a[1] + (ft + h), a[2] * a[2] + ((g + t) + h))


def combos(now, after):
    return (
        now[1] + after[1],
        after[0] - now[0],
        now[2] + after[2],
        (after[1] - now[1]) * R3,
        (now[3] + after[3]) * R3,
        (after[2] - now[2]) * R3,
        (after[3] - now[3]) * (1.0 / 3.0),
    )


def forms(parts, with_energy):
    own = [squares(p) for p in parts]
    quad = [own[0][i] + own[1][i] + own[2][i] for i in range(3)]
    for f in (cross_yz, cross_xz, cross_xy):
        quad.append(f(parts[0], parts[0]) + f(parts[1], parts[1]) + f(parts[2], parts[2]))
    if not with_energy:
        return quad, None
    x, y, z = parts
    energy = (
        MU * (quad[0] + quad[1] + quad[2])
        + (LAM + MU) * (own[0][0] + own[1][1] + own[2][2])
        + (2.0 * LAM) * (cross_xy(x, y) + cross_xz(x, z) + cross_yz(y, z))
        + (2.0 * MU) * (cross_xy(y, x) + cross_xz(z, x) + cross_yz(z, y))
    )
    return quad, energy


def bilinear(l, d):
    total = None
    diagonal = None
    for p in range(3):
        prod = [l[p][i] * d[p][i] for i in range(7)]
        ft = prod[3] + prod[6]
        three = (
            prod[0] + (ft + prod[4]),
            prod[1] + (ft + prod[5]),
            prod[2] + ((prod[4] + prod[6]) + prod[5]),
        )
        whole = three[0] + three[1] + three[2]
        total = whole if total is None else total + whole
        diagonal = three[p] if diagonal is None else diagonal + three[p]
    lx, ly, lz = l
    dx, dy, dz = d
    mixed = (
        (cross_xy(lx, dy) + cross_xy(dx, ly))
        + (cross_xz(lx, dz) + cross_xz(dx, lz))
        + (cross_yz(ly, dz) + cross_yz(dy, lz))
    )
    shear = (
        (cross_xy(dy, lx) + cross_xy(ly, dx))
        + (cross_xz(dz, lx) + cross_xz(lz, dx))
        + (cross_yz(dz, ly) + cross_yz(lz, dy))
    )
    return MU * total + (LAM + MU) * diagonal + LAM * mixed + MU * shear


def fold_rows(values):
    row = row_iota((8, LANES))
    top = row < 4
    step = [
        jnp.where(top, values[k], values[k + 4]) + roll(jnp.where(top, values[k + 4], values[k]), 4, 0)
        for k in range(4)
    ]
    top = lax.rem(row, 4) < 2
    step = [
        jnp.where(top, step[k] + roll(step[k], 6, 0), step[k + 2] + roll(step[k + 2], 2, 0)) for k in range(2)
    ]
    return jnp.where(lax.rem(row, 2) == 0, step[0] + roll(step[0], 7, 0), step[1] + roll(step[1], 1, 0))


def final_kernel(dims, full, rim, r1, r2, stress, eig, weight, sens, adjoint, yrim, zrim, sz, dz, part, w, zt, aux, cell, shear, load, stage):
    nx, ny = dims
    width = nx + 3
    tall = ny + 3
    lane = lane_iota()
    ye, ylo, yup = place("gy")

    count = GROUPS * width

    def lower(ref):
        for i in range(count):
            yrim[i, 0] = ref[2 * i]
        for c in range(GROUPS):
            yrim[count + c, 0] = ref[2 * count + c]

    def upper(ref):
        for i in range(count):
            yrim[i, 1] = ref[2 * i]
            yrim[i, 2] = ref[2 * i + 1]
        for c in range(GROUPS):
            yrim[count + c, 1] = ref[2 * count + c]

    def no_lower():
        yrim[:, 0] = jnp.zeros_like(yrim[:, 0])

    def no_upper():
        yrim[:, 1] = jnp.zeros_like(yrim[:, 1])
        yrim[:, 2] = jnp.zeros_like(yrim[:, 2])

    pick(ye, ylo, yup, r1, r2, lower, upper, no_lower, no_upper)

    @pl.loop(0, width)
    def _(x):
        for c in range(GROUPS):
            ends = roll(rim[c, x], 3)
            ends = jnp.where(lane < 3, roll(yrim[count + c, 0].astype(F32), lax.rem(2 * LANES - 16 * x, LANES)), ends)
            far = 3 * (ny + 1)
            ends = jnp.where(
                lane >= far, roll(yrim[count + c, 1].astype(F32), lax.rem(2 * LANES + far - 16 * x, LANES)), ends
            )
            for y in range(tall):
                if y == 0:
                    value = yrim[c * width + x, 0]
                elif y <= ny:
                    value = full[c, x, y - 1]
                else:
                    value = yrim[c * width + x, y - ny]
                value = value.astype(F32)
                start = 3 * tall + y
                if c < 3:
                    after = roll(value, LANES - 1)
                    after = jnp.where(lane == LANES - 1, roll(ends, LANES - 1 - (3 * y + 1)), after)
                    sz[c, x, y] = value + after
                    dz[c, x, y] = after - value
                else:
                    aux[pl.ds((x * 16 + y) * 16, 16), :] = value
                ends = jnp.where(lane == start, roll(value, start), ends)
            zrim[c, x] = ends

    def field(channel, x, first, rows):
        return aux[pl.ds((x * 16 + first) * 16 + channel, rows, stride=16), :]

    for c in range(GROUPS):
        stacked = zrim[c].reshape(width * 16, LANES)
        stacked = jnp.concatenate([stacked, jnp.zeros((LANES - width * 16, LANES), F32)], 0)
        zt[c] = stacked.T

    mode_row = lax.broadcasted_iota(jnp.int32, (MODES, LANES), 0)
    mode_lane = lax.rem(lax.broadcasted_iota(jnp.int32, (16, LANES), 1), MODES)
    eig_rows = jnp.zeros((MODES, LANES), F32)
    coef_rows = jnp.zeros((MODES, LANES), F32)
    coef_lanes = jnp.zeros((16, LANES), F32)
    for m in range(MODES):
        product = eig[m] * weight[m]
        eig_rows = jnp.where(mode_row == m, eig[m], eig_rows)
        coef_rows = jnp.where(mode_row == m, product, coef_rows)
        coef_lanes = jnp.where(mode_lane == m, product, coef_lanes)

    for x in range(nx):
        level = field(0, x + 1, 1, ny)
        density = level * (1.0 / LEVELS)
        young = 0.001 + density * density * density
        slope = 3.0 * density * density
        ratio = slope / young
        cell[6, x] = slope * (1.0 / 16.0)
        for c in range(6):
            cell[c, x] = stress[c, x] * ratio * (-1.0 / 16.0 if c < 3 else -1.0 / 8.0)

    def row_parts(x, y, h):
        found = []
        for c in range(3):
            s0 = sz[c, x, y, pl.ds(8 * h, 8), :]
            s1 = sz[c, x + 1, y, pl.ds(8 * h, 8), :]
            d0 = dz[c, x, y, pl.ds(8 * h, 8), :]
            d1 = dz[c, x + 1, y, pl.ds(8 * h, 8), :]
            found.append((s0 + s1, s1 - s0, d0 + d1, d1 - d0))
        return found

    def sweep(x, inside):
        for h in range(2):
            coef = coef_rows[8 * h : 8 * h + 8]
            now = row_parts(x, 0, h)
            for y in range(ny + 2):
                after = row_parts(x, y + 1, h)
                own = inside and 0 < y <= ny
                quad, energy = forms([combos(now[c], after[c]) for c in range(3)], own)
                if own:
                    fields = [cell[i, x - 1, pl.ds(y - 1, 1), :] for i in range(7)]
                    terms = [fields[i] * quad[i] for i in range(6)]
                    total = ((terms[0] + terms[1]) + (terms[2] + terms[3])) + (terms[4] + terms[5])
                    value = fields[6] * energy + eig_rows[8 * h : 8 * h + 8] * total
                    sens[pl.ds(8 * h * nx * ny + (x - 1) * ny + y - 1, 8, stride=nx * ny), :] = value
                for i in range(6):
                    if h == 0:
                        part[i, y] = coef * quad[i]
                    else:
                        part[i, y] += coef * quad[i]
                now = after
        for i in range(6):
            w[i, x, 0:8, 0:LANES] = fold_rows([part[i, y] for y in range(8)])
            for y in range(8, ny + 2):
                w[i, x, y : y + 1, 0:LANES] = jnp.sum(part[i, y], axis=0, keepdims=True)

    @pl.loop(1, nx + 1)
    def _(x):
        sweep(x, True)

    @pl.loop(0, 2)
    def _(i):
        sweep(i * (nx + 1), False)

    def end_nodes(c, kind, y):
        if kind == 3:
            return zt[c, pl.ds(3 * tall + y, 16), :]
        return zt[c, pl.ds(3 * y + kind, 16, stride=3), :]

    def end_parts(low, high, y):
        found = []
        for c in range(3):
            first, second = end_nodes(c, low, y), end_nodes(c, high, y)
            s, d = first + second, second - first
            s_next, d_next = roll(s, LANES - 16), roll(d, LANES - 16)
            found.append((s + s_next, s_next - s, d + d_next, d_next - d))
        return found

    sides = []
    for low, high in ((0, 3), (1, 2)):
        now, after = end_parts(low, high, 0), end_parts(low, high, 1)
        quad, _ = forms([combos(now[c], after[c]) for c in range(3)], False)
        summed = []
        for value in quad:
            value = value * coef_lanes
            for shift in (1, 2, 4, 8):
                value = value + roll(value, LANES - shift)
            summed.append(value)
        sides.append(summed)
    for i in range(6):
        both = jnp.where(lax.rem(lane, 16) == 0, sides[1][i], roll(sides[0][i], LANES - 1))
        for x in range(nx + 2):
            w[i, x, 0:16, LANES:] = roll(both, LANES - 16 * x)

    def end_field(channel, x, first, with_low):
        value = roll(zt[3, pl.ds(3 * first + 1, 16, stride=3), :], LANES - (16 * x + channel))
        if not with_low:
            return value
        low = roll(zt[3, pl.ds(3 * first, 16, stride=3), :], LANES - 1 - (16 * x + channel))
        return jnp.where(lane == 0, value, jnp.where(lane == LANES - 1, low, 0.0))

    def z_back(main, end):
        turned, turned_end = roll(main, 1), roll(end, 1)
        return jnp.where(lane == 0, turned_end, turned), jnp.where(lane == 0, turned, turned_end)

    first_rows = [None] * 6
    for x in range(nx + 2):
        level = (field(0, x, 0, 16), end_field(0, x, 0, True))
        scaled = []
        for t in range(2):
            density = level[t] * (1.0 / LEVELS)
            young = 0.001 + density * density * density
            young = jnp.where(level[t] > 0.0, young, 0.0) * (1.0 / 64.0)
            value = [w[i, x, 0:16, LANES * t : LANES * (t + 1)] * young for i in range(6)]
            trace = LAM * (value[0] + value[1] + value[2])
            scaled.append(
                [trace + (2.0 * MU) * value[i] for i in range(3)] + [(2.0 * MU) * value[i] for i in range(3, 6)]
            )
        sums, diffs = [], []
        for i in range(6):
            main, end = scaled[0][i], scaled[1][i]
            back_main, back_end = z_back(main, end)
            sums.append((main + back_main, end + back_end))
            diffs.append((main - back_main, end - back_end))
        xx, yy, zz, yz, xz, xy = range(6)
        for slot, source in enumerate((sums[xx], sums[xy], diffs[xz], sums[yy], diffs[yz], sums[xz], sums[yz], diffs[zz])):
            for t in range(2):
                shear[slot, t, 0:16] = source[t]
        rows = []
        for t in range(2):
            low = [shear[slot, t, 0:16] for slot in range(8)]
            high = [shear[slot, t, 1:17] for slot in range(8)]
            plus = lambda k: low[k] + high[k]
            minus = lambda k: high[k] - low[k]
            rows.append(
                [
                    plus(0),
                    minus(1) + plus(2),
                    plus(1),
                    minus(3) + plus(4),
                    plus(5),
                    minus(6) + plus(7),
                ]
            )
        if x > 0:
            node = x - 1
            for t in range(2):
                free = field(1, x, 1, 16) if t == 0 else end_field(1, x, 1, False)
                for p in range(3):
                    value = (rows[t][2 * p] - first_rows[t][2 * p]) + (rows[t][2 * p + 1] + first_rows[t][2 * p + 1])
                    load[p, node, t] = value * free
                    if t == 0:
                        shift = field(2 + p, x, 1, 16) + field(5 + p, x, 1, 16)
                    else:
                        shift = end_field(2 + p, x, 1, False) + end_field(5 + p, x, 1, False)
                    load[3 + p, node, t] = shift
        first_rows = rows

    def node_layer(x):
        found = []
        for f in range(6):
            main, end = load[f, x, 0], load[f, x, 1]
            after = jnp.where(lane == LANES - 1, roll(end, LANES - 1), roll(main, LANES - 1))
            s, d = main + after, after - main
            stage[0, 0:16] = s
            stage[1, 0:16] = d
            s_next, d_next = stage[0, 1:9], stage[1, 1:9]
            s, d = s[0:8], d[0:8]
            found.append((s + s_next, s_next - s, d + d_next, d_next - d))
        return found

    def layer_combos(now, after):
        return (
            after[0] - now[0],
            now[1] + after[1],
            now[2] + after[2],
            (after[1] - now[1]) * R3,
            (after[2] - now[2]) * R3,
            (now[3] + after[3]) * R3,
            (after[3] - now[3]) * (1.0 / 3.0),
        )

    now = node_layer(0)
    for x in range(nx):
        after = node_layer(x + 1)
        parts = [layer_combos(now[f], after[f]) for f in range(6)]
        adjoint[x] = cell[6, x] * bilinear(parts[:3], parts[3:])
        now = after


def partner(index, size, kind):
    other = index ^ 1 if kind == 1 else ((index + 1) ^ 1) - 1
    return other if 0 <= other < size else None


def swap(block, axes, kinds, fill):
    sizes = [lax.axis_size(a) for a in axes]
    route = []
    for i in range(sizes[0]):
        for j in range(sizes[1]):
            ends = [p if k == 0 else partner(p, n, k) for p, n, k in zip((i, j), sizes, kinds, strict=True)]
            if ends[0] is None:
                ends = [i, partner(j, sizes[1], 1)] if fill else None
            elif ends[1] is None:
                ends = [partner(i, sizes[0], 1) if kinds[0] == 0 else ends[0], j] if fill else None
            if ends is not None:
                route.append((i * sizes[1] + j, ends[0] * sizes[1] + ends[1]))
    return lax.ppermute(block, axes, route)


def vmem(n):
    return [pl.BlockSpec(memory_space=pltpu.VMEM)] * n


def body(mode_shapes, stress_field, displacement, material, fixed_nodes, eigenvalues, mode_weight):
    nx, ny, nz = material.shape
    dims = (nx, ny)
    width = nx + 3
    tall = ny + 3
    sds = jax.ShapeDtypeStruct
    tile = (MODES, LANES)
    tiles, x1, x2, edge, ex1, ex2 = pl.pallas_call(
        functools.partial(pack_kernel, dims),
        out_shape=(
            sds((GROUPS, nx, ny) + tile, BF16),
            sds((GROUPS, 2, ny) + tile, BF16),
            sds((GROUPS, 2, ny) + tile, BF16),
            sds((GROUPS, nx) + tile, BF16),
            sds((GROUPS, 2) + tile, BF16),
            sds((GROUPS, 2) + tile, BF16),
        ),
        in_specs=vmem(4),
        out_specs=tuple(vmem(6)),
        scratch_shapes=[pltpu.VMEM((GROUPS * MODES * nx * ny, LANES), F32)],
        compiler_params=pltpu.CompilerParams(vmem_limit_bytes=8 << 20),
        name="pack",
    )(mode_shapes, material, fixed_nodes, displacement)

    xz = ("gx", "gz")
    zkinds = (1,) if lax.axis_size("gz") == 2 else (1, 2)
    r1 = swap(x1, xz, (1, 0), True)
    r2 = swap(x2, xz, (2, 0), True)
    rz = [swap(edge, xz, (0, k), True) for k in zkinds]
    rz1 = [swap(ex1, xz, (1, k), True) for k in zkinds]
    rz2 = [swap(ex2, xz, (2, k), True) for k in zkinds]
    count = GROUPS * width * 2 + GROUPS
    full, rim, y1, y2 = pl.pallas_call(
        functools.partial(merge_kernel, dims, len(zkinds)),
        out_shape=(
            sds((GROUPS, width, ny) + tile, BF16),
            sds((GROUPS, width) + tile, F32),
            sds((count,) + tile, BF16),
            sds((count,) + tile, BF16),
        ),
        in_specs=vmem(3 + 3 * len(zkinds)),
        out_specs=tuple(vmem(4)),
        compiler_params=pltpu.CompilerParams(vmem_limit_bytes=8 << 20),
        name="merge",
    )(tiles, r1, r2, *rz, *rz1, *rz2)

    yz = ("gy", "gz")
    ry1 = swap(y1, yz, (1, 0), True)
    ry2 = swap(y2, yz, (2, 0), True)
    sens, adjoint = pl.pallas_call(
        functools.partial(final_kernel, dims),
        out_shape=(sds((MODES * nx * ny, LANES), F32), sds((nx, ny, LANES), F32)),
        in_specs=vmem(5) + [pl.BlockSpec(memory_space=pltpu.SMEM)] * 2,
        out_specs=tuple(vmem(2)),
        scratch_shapes=[
            pltpu.VMEM((GROUPS * width + GROUPS, 3) + tile, BF16),
            pltpu.VMEM((GROUPS, width) + tile, F32),
            pltpu.VMEM((3, width, tall) + tile, F32),
            pltpu.VMEM((3, width, tall) + tile, F32),
            pltpu.VMEM((6, ny + 2, 8, LANES), F32),
            pltpu.VMEM((6, nx + 2, 16, 2 * LANES), F32),
            pltpu.VMEM((GROUPS, LANES, LANES), F32),
            pltpu.VMEM(((width + 1) * 16 * 16, LANES), F32),
            pltpu.VMEM((7, nx, ny, LANES), F32),
            pltpu.VMEM((8, 2, 24, LANES), F32),
            pltpu.VMEM((6, nx + 1, 2, 16, LANES), F32),
            pltpu.VMEM((2, 24, LANES), F32),
        ],
        compiler_params=pltpu.CompilerParams(vmem_limit_bytes=32 << 20),
        name="finish",
    )(full, rim, ry1, ry2, stress_field, eigenvalues, mode_weight)
    return sens.reshape(MODES, nx, ny, nz), adjoint


def solution(mesh):
    return jax.shard_map(
        body,
        mesh=mesh,
        in_specs=(
            P(None, None, "gx", "gy", "gz"),
            P(None, "gx", "gy", "gz"),
            P(None, "gx", "gy", "gz"),
            P("gx", "gy", "gz"),
            P("gx", "gy", "gz"),
            P(),
            P(),
        ),
        out_specs=(P(None, "gx", "gy", "gz"), P("gx", "gy", "gz")),
        check_vma=False,
    )
```

```python
import functools
import math

import jax
import jax.numpy as jnp
from jax import lax
from jax.experimental import pallas as pl
from jax.experimental.pallas import tpu as pltpu
from jax.sharding import PartitionSpec as P

LEVELS = 8
POISSON = 0.45
LAM = POISSON / ((1.0 + POISSON) * (1.0 - 2.0 * POISSON))
MU = 0.5 / (1.0 + POISSON)
R3 = 1.0 / math.sqrt(3.0)
F32 = jnp.float32
BF16 = jnp.bfloat16
MODES = 16
GROUPS = 4
LANES = 128


def lane_iota(shape=(MODES, LANES)):
    return lax.broadcasted_iota(jnp.int32, shape, len(shape) - 1)


def row_iota(shape):
    return lax.broadcasted_iota(jnp.int32, shape, 0)


def roll(value, shift, axis=1):
    size = value.shape[axis]
    if isinstance(shift, int):
        shift = shift % size
        if shift == 0:
            return value
    return pltpu.roll(value, shift, axis)


def place(axis):
    me = lax.axis_index(axis)
    size = lax.axis_size(axis)
    even = lax.rem(me, 2) == 0
    return even, me > 0, me < size - 1


HALF = 8
PITCH = 40


def pair_up(first, second):
    return jnp.concatenate([first[:HALF].astype(F32), second[:HALF].astype(F32)], 0).astype(BF16)


def pack_kernel(dims, modes_in, material_in, fixed_in, disp_in, tiles, x1, x2, edge, ex1, ex2, modes, material, fixed, disp, raw, sems):
    nx, ny = dims
    copies = [
        pltpu.make_async_copy(src, dst, sems.at[i])
        for i, (src, dst) in enumerate(
            [(modes_in.at[c], modes.at[c]) for c in range(3)]
            + [(material_in, material), (fixed_in, fixed), (disp_in, disp)]
        )
    ]
    for copy in copies:
        copy.start()
    part = nx * ny

    def store(c, m, value):
        start = (c * MODES + m) * PITCH
        raw[start : start + part, :] = value.reshape(part, LANES)

    def spread(c):
        @pl.loop(0, nx)
        def _(x):
            for y in range(ny):
                value = raw[pl.ds(c * MODES * PITCH + x * ny + y, MODES, stride=PITCH), :]
                tiles[c, x, y] = value.astype(BF16)

    for c in range(3):
        copies[c].wait()
        for m in range(MODES):
            store(c, m, modes[c, m].astype(F32))
        spread(c)
    for copy in copies[3:]:
        copy.wait()
    store(3, 0, material[...].astype(F32) + 1.0)
    store(3, 1, 1.0 - fixed[...].astype(F32))
    for c in range(3):
        value = disp[c]
        first = value.astype(BF16).astype(F32)
        store(3, 2 + c, first)
        store(3, 5 + c, value - first)
    for m in range(HALF, MODES):
        store(3, m, jnp.zeros((part, LANES), F32))
    spread(3)

    col = lane_iota((LANES, LANES))
    kind = lax.rem(col, 3)
    wanted = row_iota((LANES, LANES)) == jnp.where(kind == 0, LANES - 1, kind - 1)
    ends = None
    for y in range(ny):
        chosen = jnp.where(wanted & (col >= 3 * y) & (col < 3 * y + 3), 1.0, 0.0).astype(BF16)
        block = tiles[:, :, y].reshape(GROUPS * nx * MODES, LANES)
        term = jnp.dot(block, chosen, preferred_element_type=F32)
        ends = term if ends is None else ends + term
    ends = ends.reshape(GROUPS, nx, MODES, LANES)
    pieces = LANES // nx
    even, _, _ = place("gx")
    last = [ends[c, nx - 1] for c in range(GROUPS)]
    for c in range(GROUPS):
        total = ends[c, 0]
        for x in range(1, nx):
            total = total + roll(ends[c, x], pieces * x)
        edge[c] = total.astype(BF16)
    for out, out_edge, upward in ((x1, ex1, even), (x2, ex2, jnp.logical_not(even))):
        flag = upward.astype(F32)
        for s in range(2):
            layer = jnp.where(upward, nx - 1, s)
            for c in range(3):
                for y in range(ny):
                    out[(c * 2 + s) * ny + y] = tiles[c, layer, y]
        layer = jnp.where(upward, nx - 1, 0)
        for y in range(0, ny, 2):
            out[6 * ny + y // 2] = pair_up(tiles[3, layer, y], tiles[3, layer, y + 1])
        for c in range(GROUPS):
            below = ends[c, 0] + roll(ends[c, 1], pieces)
            out_edge[c] = (last[c] * flag + below * (1.0 - flag)).astype(BF16)


def pick(parity, lower, upper, first, second, use_lower, use_upper, none_lower, none_upper):
    odd = jnp.logical_not(parity)
    pl.when(jnp.logical_and(lower, parity))(lambda: use_lower(second))
    pl.when(jnp.logical_and(lower, odd))(lambda: use_lower(first))
    pl.when(jnp.logical_and(upper, parity))(lambda: use_upper(first))
    pl.when(jnp.logical_and(upper, odd))(lambda: use_upper(second))
    pl.when(jnp.logical_not(lower))(none_lower)
    pl.when(jnp.logical_not(upper))(none_upper)


def merge_kernel(dims, zcount, *refs):
    nx, ny = dims
    tiles, r1, r2 = refs[:3]
    rz = refs[3 : 3 + zcount]
    rz1 = refs[3 + zcount : 3 + 2 * zcount]
    rz2 = refs[3 + 2 * zcount : 3 + 3 * zcount]
    rim, y1, y2, rows_aux = refs[3 + 3 * zcount :]
    xe, xlo, xup = place("gx")
    ze, zlo, zup = place("gz")
    ye, _, _ = place("gy")
    width = nx + 3
    pieces = LANES // nx
    lane = lane_iota()
    phase = lax.rem(lane, 3)
    kept = lane < 3 * ny
    even_f = ze.astype(F32)
    low_mask = jnp.where(kept & (phase == 0), zlo.astype(F32), 0.0)
    high_mask = jnp.where(kept & (phase != 0), zup.astype(F32), 0.0)
    whole = low_mask + high_mask

    def merged(blocks, slot):
        turned = [roll(b.astype(F32), LANES - pieces * slot) for b in blocks]
        if len(turned) == 1:
            return turned[0] * whole
        first, second = turned
        low = second * even_f + first * (1.0 - even_f)
        high = first * even_f + second * (1.0 - even_f)
        return low * low_mask + high * high_mask

    for c in range(GROUPS):
        for x in range(nx):
            rim[c, x + 1] = merged([r[c] for r in rz], x)

        def rim_lower(refs, c=c):
            rim[c, 0] = merged([r[c] for r in refs], 0)

        def rim_upper(refs, c=c):
            for s in range(2):
                rim[c, nx + 1 + s] = merged([r[c] for r in refs], s)

        def rim_no_lower(c=c):
            rim[c, 0] = jnp.zeros((MODES, LANES), F32)

        def rim_no_upper(c=c):
            for s in range(2):
                rim[c, nx + 1 + s] = jnp.zeros((MODES, LANES), F32)

        pick(xe, xlo, xup, rz1, rz2, rim_lower, rim_upper, rim_no_lower, rim_no_upper)

    blank = jnp.zeros((MODES, LANES), BF16)
    blank_half = jnp.zeros((HALF, LANES), F32)

    def half_of(ref, row):
        pairs = ref[6 * ny + row // 2].astype(F32)
        odd = lax.rem(row, 2).astype(F32)
        return pairs[:HALF] * (1.0 - odd) + pairs[HALF:] * odd

    for out, upward in ((y1, ye), (y2, jnp.logical_not(ye))):
        rows = [jnp.where(upward, ny - 1, s) for s in range(2)]
        for c in range(3):
            for s in range(2):
                for x in range(nx):
                    out[(c * width + x + 1) * 2 + s] = tiles[c, x, rows[s]]
        for x in range(nx):
            rows_aux[x + 1] = tiles[3, x, rows[0]][:HALF].astype(F32)

        def lower(ref, out=out, rows=rows):
            for c in range(3):
                for s in range(2):
                    out[c * width * 2 + s] = ref[c * 2 * ny + rows[s]]
            rows_aux[0] = half_of(ref, rows[0])

        def upper(ref, out=out, rows=rows):
            for c in range(3):
                for t in range(2):
                    for s in range(2):
                        out[(c * width + nx + 1 + t) * 2 + s] = ref[(c * 2 + t) * ny + rows[s]]
            rows_aux[nx + 1] = half_of(ref, rows[0])

        def no_lower(out=out):
            for c in range(3):
                for s in range(2):
                    out[c * width * 2 + s] = blank
            rows_aux[0] = blank_half

        def no_upper(out=out):
            for c in range(3):
                for i in range(4):
                    out[(c * width + nx + 1) * 2 + i] = blank
            rows_aux[nx + 1] = blank_half

        pick(xe, xlo, xup, r1, r2, lower, upper, no_lower, no_upper)
        base = 6 * width
        for x in range(0, nx + 2, 2):
            out[base + x // 2] = jnp.concatenate([rows_aux[x], rows_aux[x + 1]], 0).astype(BF16)
        base += (nx + 2) // 2
        for c in range(GROUPS):
            ends = jnp.zeros((MODES, LANES), F32)
            for x in range(width):
                start = 16 * x
                turned = roll(rim[c, x], lax.rem(start + LANES - 3 * rows[0], LANES))
                ends = jnp.where((lane >= start) & (lane < start + 6), turned, ends)
            out[base + c] = ends.astype(BF16)


def cross_xy(a, b):
    return a[0] * b[1] + a[4] * b[5]


def cross_xz(a, b):
    return a[0] * b[2] + a[3] * b[5]


def cross_yz(a, b):
    return a[1] * b[2] + a[3] * b[4]


def squares(a):
    f, g, h, t = a[3] * a[3], a[4] * a[4], a[5] * a[5], a[6] * a[6]
    ft = f + t
    return (a[0] * a[0] + (ft + g), a[1] * a[1] + (ft + h), a[2] * a[2] + ((g + t) + h))


def combos(now, after):
    return (
        now[1] + after[1],
        after[0] - now[0],
        now[2] + after[2],
        (after[1] - now[1]) * R3,
        (now[3] + after[3]) * R3,
        (after[2] - now[2]) * R3,
        (after[3] - now[3]) * (1.0 / 3.0),
    )


def forms(parts, with_energy):
    own = [squares(p) for p in parts]
    quad = [own[0][i] + own[1][i] + own[2][i] for i in range(3)]
    for f in (cross_yz, cross_xz, cross_xy):
        quad.append(f(parts[0], parts[0]) + f(parts[1], parts[1]) + f(parts[2], parts[2]))
    if not with_energy:
        return quad, None
    x, y, z = parts
    energy = (
        MU * (quad[0] + quad[1] + quad[2])
        + (LAM + MU) * (own[0][0] + own[1][1] + own[2][2])
        + (2.0 * LAM) * (cross_xy(x, y) + cross_xz(x, z) + cross_yz(y, z))
        + (2.0 * MU) * (cross_xy(y, x) + cross_xz(z, x) + cross_yz(z, y))
    )
    return quad, energy


def bilinear(l, d):
    total = None
    diagonal = None
    for p in range(3):
        prod = [l[p][i] * d[p][i] for i in range(7)]
        ft = prod[3] + prod[6]
        three = (
            prod[0] + (ft + prod[4]),
            prod[1] + (ft + prod[5]),
            prod[2] + ((prod[4] + prod[6]) + prod[5]),
        )
        whole = three[0] + three[1] + three[2]
        total = whole if total is None else total + whole
        diagonal = three[p] if diagonal is None else diagonal + three[p]
    lx, ly, lz = l
    dx, dy, dz = d
    mixed = (
        (cross_xy(lx, dy) + cross_xy(dx, ly))
        + (cross_xz(lx, dz) + cross_xz(dx, lz))
        + (cross_yz(ly, dz) + cross_yz(dy, lz))
    )
    shear = (
        (cross_xy(dy, lx) + cross_xy(ly, dx))
        + (cross_xz(dz, lx) + cross_xz(lz, dx))
        + (cross_yz(dz, ly) + cross_yz(lz, dy))
    )
    return MU * total + (LAM + MU) * diagonal + LAM * mixed + MU * shear


def fold_rows(values):
    row = row_iota((8, LANES))
    top = row < 4
    step = [
        jnp.where(top, values[k], values[k + 4]) + roll(jnp.where(top, values[k + 4], values[k]), 4, 0)
        for k in range(4)
    ]
    top = lax.rem(row, 4) < 2
    step = [
        jnp.where(top, step[k] + roll(step[k], 6, 0), step[k + 2] + roll(step[k + 2], 2, 0)) for k in range(2)
    ]
    return jnp.where(lax.rem(row, 2) == 0, step[0] + roll(step[0], 7, 0), step[1] + roll(step[1], 1, 0))


def z_table(kind):
    row = row_iota((2 * LANES, 2 * LANES))
    col = lane_iota((2 * LANES, 2 * LANES))
    z = jnp.where(col < LANES, col, col - LANES)
    own = jnp.where(row == z, jnp.where(col < LANES, 1.0, -1.0), 0.0)
    after = jnp.where((row == z + 1) & (row < LANES), 1.0, 0.0)
    rim = jnp.where((z == LANES - 1) & (row == LANES + kind), 1.0, 0.0)
    return (own + after + rim).astype(BF16)


def first_column(lane_to):
    return jnp.where((row_iota((LANES, LANES)) == 0) & (lane_iota((LANES, LANES)) == lane_to), 1.0, 0.0).astype(BF16)


def rows_along_z(block, rim, kind, sz, dz, at):
    both = jnp.dot(jnp.concatenate([block, rim], 1), z_table(kind), preferred_element_type=F32)
    sz[at] = both[:, :LANES].reshape(sz.shape[1:])
    dz[at] = both[:, LANES:].reshape(dz.shape[1:])


def x_parts(sz, dz, y, x, h):
    found = []
    for c in range(3):
        s0 = sz[y, c, x, pl.ds(8 * h, 8), :]
        s1 = sz[y, c, x + 1, pl.ds(8 * h, 8), :]
        d0 = dz[y, c, x, pl.ds(8 * h, 8), :]
        d1 = dz[y, c, x + 1, pl.ds(8 * h, 8), :]
        found.append((s0 + s1, s1 - s0, d0 + d1, d1 - d0))
    return found


def mode_value(quad, energy, fields, eig_rows):
    terms = [fields[i] * quad[i] for i in range(6)]
    total = ((terms[0] + terms[1]) + (terms[2] + terms[3])) + (terms[4] + terms[5])
    return fields[6] * energy + eig_rows * total


FIELDS = 5


def inner_kernel(dims, tiles, r1, r2, rim, stress, eig, weight, sens, wmain, field, cell, zr, scale, full, sz, dz, part, aux):
    nx, ny = dims
    width = nx + 3
    tall = ny + 3
    lane = lane_iota()
    xe, xlo, xup = place("gx")

    full[:, 1 : nx + 1] = tiles[0:3]
    for x in range(nx):
        for y in range(ny):
            aux[((x + 1) * ny + y) * HALF : ((x + 1) * ny + y + 1) * HALF, :] = tiles[3, x, y][:HALF].astype(F32)

    def halves(ref, x):
        for i in range(ny // 2):
            start = (x * ny + 2 * i) * HALF
            aux[start : start + 2 * HALF, :] = ref[6 * ny + i].astype(F32)

    def lower(ref):
        for c in range(3):
            for y in range(ny):
                full[c, 0, y] = ref[c * 2 * ny + y]
        halves(ref, 0)

    def upper(ref):
        for c in range(3):
            for s in range(2):
                for y in range(ny):
                    full[c, nx + 1 + s, y] = ref[(c * 2 + s) * ny + y]
        halves(ref, nx + 1)

    def no_lower():
        full[:, 0:1] = jnp.zeros((3, 1, ny, MODES, LANES), BF16)
        aux[0 : ny * HALF, :] = jnp.zeros((ny * HALF, LANES), F32)

    def no_upper():
        full[:, nx + 1 : nx + 3] = jnp.zeros((3, 2, ny, MODES, LANES), BF16)
        aux[(nx + 1) * ny * HALF : (nx + 2) * ny * HALF, :] = jnp.zeros((ny * HALF, LANES), F32)

    pick(xe, xlo, xup, r1, r2, lower, upper, no_lower, no_upper)

    count = 3 * width * MODES
    ends = rim[0:3].reshape(count, LANES).astype(BF16)
    column = None
    for y in range(ny):
        block = full[:, :, y].reshape(count, LANES)
        rows_along_z(block, ends, 3 * y + 1, sz, dz, y)
        term = jnp.dot(block, first_column(3 * tall + y + 1), preferred_element_type=F32)
        column = term if column is None else column + term
    column = column.reshape(3, width, MODES, LANES)
    for c in range(GROUPS):
        for x in range(width):
            turned = roll(rim[c, x], 3)
            zr[c, x] = turned + column[c, x] if c < 3 else turned

    for x in range(nx + 2):
        def channel(k):
            return aux[pl.ds(x * ny * HALF + k, ny, stride=HALF), :]

        field[0, x] = channel(0)
        field[1, x] = channel(1)
        for c in range(3):
            field[2 + c, x] = channel(2 + c) + channel(5 + c)

    mode_row = row_iota((MODES, LANES))
    mode_lane = lax.rem(lane, MODES)
    eig_rows = jnp.zeros((MODES, LANES), F32)
    coef_rows = jnp.zeros((MODES, LANES), F32)
    coef_lanes = jnp.zeros((MODES, LANES), F32)
    for m in range(MODES):
        product = eig[m] * weight[m]
        eig_rows = jnp.where(mode_row == m, eig[m], eig_rows)
        coef_rows = jnp.where(mode_row == m, product, coef_rows)
        coef_lanes = jnp.where(mode_lane == m, product, coef_lanes)
    scale[0], scale[1], scale[2] = eig_rows, coef_rows, coef_lanes

    for x in range(nx):
        density = field[0, x + 1] * (1.0 / LEVELS)
        young = 0.001 + density * density * density
        slope = 3.0 * density * density
        ratio = slope / young
        cell[6, x] = slope * (1.0 / 16.0)
        for c in range(6):
            cell[c, x] = stress[c, x] * ratio * (-1.0 / 16.0 if c < 3 else -1.0 / 8.0)

    def sweep(x, inside):
        for h in range(2):
            coef = scale[1, 8 * h : 8 * h + 8]
            eig_half = scale[0, 8 * h : 8 * h + 8]
            now = x_parts(sz, dz, 0, x, h)
            for y in range(ny - 1):
                after = x_parts(sz, dz, y + 1, x, h)
                quad, energy = forms([combos(now[c], after[c]) for c in range(3)], inside)
                if inside:
                    fields = [cell[i, x - 1, pl.ds(y, 1), :] for i in range(7)]
                    start = 8 * h * nx * ny + (x - 1) * ny + y
                    sens[pl.ds(start, 8, stride=nx * ny), :] = mode_value(quad, energy, fields, eig_half)
                for i in range(6):
                    if h == 0:
                        part[i, y] = coef * quad[i]
                    else:
                        part[i, y] += coef * quad[i]
                now = after
        blank = jnp.zeros((8, LANES), F32)
        for i in range(6):
            wmain[i, x] = fold_rows([blank] + [part[i, y] for y in range(ny - 1)])

    @pl.loop(1, nx + 1)
    def _(x):
        sweep(x, True)

    @pl.loop(0, 2)
    def _(i):
        sweep(i * (nx + 1), False)


def final_kernel(dims, y1, y2, r1, r2, rim, wmain, field_in, cell, zr, scale, sens_in, sens, adjoint, rows, rows_aux, rows_end, sz, dz, sum_z, w, zt, field, shear, load, stage, last, sems):
    del sens_in
    nx, ny = dims
    width = nx + 3
    tall = ny + 3
    lane = lane_iota()
    ye, ylo, yup = place("gy")

    def copy_rows(to, ref, slot):
        for i in range(3 * width):
            rows[to, i] = ref[2 * i + slot]

    aux_base = 6 * width
    end_base = aux_base + (nx + 2) // 2

    def copy_aux(to, ref):
        for i in range((nx + 2) // 2):
            rows_aux[to, i] = ref[aux_base + i].astype(F32)
        for c in range(GROUPS):
            rows_end[to, c] = ref[end_base + c].astype(F32)

    def lower(ref):
        copy_rows(0, ref, 0)
        copy_aux(0, ref)

    def upper(ref):
        copy_rows(3, ref, 0)
        copy_rows(4, ref, 1)
        copy_aux(1, ref)

    def no_lower():
        rows[0] = jnp.zeros_like(rows[0])
        rows_aux[0] = jnp.zeros_like(rows_aux[0])
        rows_end[0] = jnp.zeros_like(rows_end[0])

    def no_upper():
        rows[3:5] = jnp.zeros_like(rows[3:5])
        rows_aux[1] = jnp.zeros_like(rows_aux[1])
        rows_end[1] = jnp.zeros_like(rows_end[1])

    pick(ye, ylo, yup, r1, r2, lower, upper, no_lower, no_upper)

    @pl.when(ye)
    def _():
        copy_rows(2, y1, 0)
        copy_rows(1, y2, 0)

    @pl.when(jnp.logical_not(ye))
    def _():
        copy_rows(2, y2, 0)
        copy_rows(1, y1, 0)

    far = 3 * (ny + 1)
    count = 3 * width * MODES
    at = (0, 1, ny, ny + 1, ny + 2)
    column = None
    for i in (0, 3, 4):
        term = jnp.dot(rows[i].reshape(count, LANES), first_column(3 * tall + at[i]), preferred_element_type=F32)
        column = term if column is None else column + term
    column = column.reshape(3, width, MODES, LANES)
    full_rim = []
    for c in range(GROUPS):
        layers = []
        for x in range(width):
            ends = jnp.where(lane < 3, roll(rows_end[0, c], LANES - 16 * x), zr[c, x])
            ends = jnp.where((lane >= far) & (lane < far + 6), roll(rows_end[1, c], far - 16 * x), ends)
            if c < 3:
                ends = ends + column[c, x]
            layers.append(ends)
        layers.append(jnp.zeros((LANES - width * MODES, LANES), F32))
        stacked = jnp.concatenate(layers, 0)
        full_rim.append(stacked[: width * MODES])
        zt[c] = stacked.T
    ends = jnp.concatenate(full_rim[:3], 0).astype(BF16)
    for i in range(5):
        rows_along_z(rows[i].reshape(count, LANES), ends, 3 * at[i] + 1, sz, dz, i)

    w[:, :, 0:8, 0:LANES] = wmain[...]

    def sweep(x, inside):
        for h in range(2):
            coef = scale[1, 8 * h : 8 * h + 8]
            now = None
            for i, (first, own) in enumerate(((0, False), (2, inside), (3, False))):
                if i < 2:
                    now = x_parts(sz, dz, first, x, h)
                after = x_parts(sz, dz, first + 1, x, h)
                quad, energy = forms([combos(now[c], after[c]) for c in range(3)], own)
                if own:
                    fields = [cell[k, x - 1, ny - 1 : ny, :] for k in range(7)]
                    last[x - 1, pl.ds(8 * h, 8), :] = mode_value(quad, energy, fields, scale[0, 8 * h : 8 * h + 8])
                for k in range(6):
                    if h == 0:
                        sum_z[k, i] = coef * quad[k]
                    else:
                        total = jnp.sum(sum_z[k, i] + coef * quad[k], axis=0, keepdims=True)
                        row = (0, ny, ny + 1)[i]
                        w[k, x, row : row + 1, 0:LANES] = total
                now = after

    @pl.loop(1, nx + 1)
    def _(x):
        sweep(x, True)

    @pl.loop(0, 2)
    def _(i):
        sweep(i * (nx + 1), False)

    copies = [pltpu.make_async_copy(last.at[x], sens.at[:, x, ny - 1], sems.at[x]) for x in range(nx)]
    for copy in copies:
        copy.start()

    for x in range(nx + 2):
        for k in range(FIELDS):
            field[k, x, 1 : ny + 1] = field_in[k, x]
        for side, row in ((0, 0), (1, ny + 1)):
            pair = rows_aux[side, x // 2][(x % 2) * HALF : (x % 2 + 1) * HALF]
            field[0, x, row : row + 1] = pair[0:1]
            field[1, x, row : row + 1] = pair[1:2]
            for c in range(3):
                field[2 + c, x, row : row + 1] = pair[2 + c : 3 + c] + pair[5 + c : 6 + c]

    def end_nodes(c, kind, y):
        if kind == 3:
            return zt[c, pl.ds(3 * tall + y, 16), :]
        return zt[c, pl.ds(3 * y + kind, 16, stride=3), :]

    def end_parts(low, high, y):
        found = []
        for c in range(3):
            first, second = end_nodes(c, low, y), end_nodes(c, high, y)
            s, d = first + second, second - first
            s_next, d_next = roll(s, LANES - 16), roll(d, LANES - 16)
            found.append((s + s_next, s_next - s, d + d_next, d_next - d))
        return found

    sides = []
    for low, high in ((0, 3), (1, 2)):
        now, after = end_parts(low, high, 0), end_parts(low, high, 1)
        quad, _ = forms([combos(now[c], after[c]) for c in range(3)], False)
        summed = []
        for value in quad:
            value = value * scale[2]
            for shift in (1, 2, 4, 8):
                value = value + roll(value, LANES - shift)
            summed.append(value)
        sides.append(summed)
    for i in range(6):
        both = jnp.where(lax.rem(lane, 16) == 0, sides[1][i], roll(sides[0][i], LANES - 1))
        for x in range(nx + 2):
            w[i, x, 0:16, LANES:] = roll(both, LANES - 16 * x)

    def end_field(channel, x, first, with_low):
        value = roll(zt[3, pl.ds(3 * first + 1, 16, stride=3), :], LANES - (16 * x + channel))
        if not with_low:
            return value
        low = roll(zt[3, pl.ds(3 * first, 16, stride=3), :], LANES - 1 - (16 * x + channel))
        return jnp.where(lane == 0, value, jnp.where(lane == LANES - 1, low, 0.0))

    def z_back(main, end):
        turned, turned_end = roll(main, 1), roll(end, 1)
        return jnp.where(lane == 0, turned_end, turned), jnp.where(lane == 0, turned, turned_end)

    first_rows = None
    for x in range(nx + 2):
        level = (field[0, x, 0:16], end_field(0, x, 0, True))
        scaled = []
        for t in range(2):
            density = level[t] * (1.0 / LEVELS)
            young = 0.001 + density * density * density
            young = jnp.where(level[t] > 0.0, young, 0.0) * (1.0 / 64.0)
            value = [w[i, x, 0:16, LANES * t : LANES * (t + 1)] * young for i in range(6)]
            trace = LAM * (value[0] + value[1] + value[2])
            scaled.append(
                [trace + (2.0 * MU) * value[i] for i in range(3)] + [(2.0 * MU) * value[i] for i in range(3, 6)]
            )
        sums, diffs = [], []
        for i in range(6):
            main, end = scaled[0][i], scaled[1][i]
            back_main, back_end = z_back(main, end)
            sums.append((main + back_main, end + back_end))
            diffs.append((main - back_main, end - back_end))
        xx, yy, zz, yz, xz, xy = range(6)
        order = (sums[xx], sums[xy], diffs[xz], sums[yy], diffs[yz], sums[xz], sums[yz], diffs[zz])
        for slot, source in enumerate(order):
            for t in range(2):
                shear[slot, t, 0:16] = source[t]
        found = []
        for t in range(2):
            low = [shear[slot, t, 0:16] for slot in range(8)]
            high = [shear[slot, t, 1:17] for slot in range(8)]
            plus = [low[k] + high[k] for k in range(8)]
            minus = [high[k] - low[k] for k in range(8)]
            found.append([plus[0], minus[1] + plus[2], plus[1], minus[3] + plus[4], plus[5], minus[6] + plus[7]])
        if x > 0:
            node = x - 1
            for t in range(2):
                free = field[1, x, 1:17] if t == 0 else end_field(1, x, 1, False)
                for p in range(3):
                    value = (found[t][2 * p] - first_rows[t][2 * p]) + (
                        found[t][2 * p + 1] + first_rows[t][2 * p + 1]
                    )
                    load[p, node, t] = value * free
                    if t == 0:
                        shift = field[2 + p, x, 1:17]
                    else:
                        shift = end_field(2 + p, x, 1, False) + end_field(5 + p, x, 1, False)
                    load[3 + p, node, t] = shift
        first_rows = found

    def node_layer(x):
        found = []
        for f in range(6):
            main, end = load[f, x, 0], load[f, x, 1]
            after = jnp.where(lane == LANES - 1, roll(end, LANES - 1), roll(main, LANES - 1))
            s, d = main + after, after - main
            stage[0, 0:16] = s
            stage[1, 0:16] = d
            s_next, d_next = stage[0, 1:9], stage[1, 1:9]
            s, d = s[0:8], d[0:8]
            found.append((s + s_next, s_next - s, d + d_next, d_next - d))
        return found

    def layer_combos(now, after):
        return (
            after[0] - now[0],
            now[1] + after[1],
            now[2] + after[2],
            (after[1] - now[1]) * R3,
            (after[2] - now[2]) * R3,
            (now[3] + after[3]) * R3,
            (after[3] - now[3]) * (1.0 / 3.0),
        )

    now = node_layer(0)
    for x in range(nx):
        after = node_layer(x + 1)
        parts = [layer_combos(now[f], after[f]) for f in range(6)]
        adjoint[x] = cell[6, x] * bilinear(parts[:3], parts[3:])
        now = after
    for copy in copies:
        copy.wait()


def partner(index, size, kind):
    other = index ^ 1 if kind == 1 else ((index + 1) ^ 1) - 1
    return other if 0 <= other < size else None


def swap(block, axes, kinds, fill):
    sizes = [lax.axis_size(a) for a in axes]
    route = []
    for i in range(sizes[0]):
        for j in range(sizes[1]):
            ends = [p if k == 0 else partner(p, n, k) for p, n, k in zip((i, j), sizes, kinds, strict=True)]
            if ends[0] is None:
                ends = [i, partner(j, sizes[1], 1)] if fill else None
            elif ends[1] is None:
                ends = [partner(i, sizes[0], 1) if kinds[0] == 0 else ends[0], j] if fill else None
            if ends is not None:
                route.append((i * sizes[1] + j, ends[0] * sizes[1] + ends[1]))
    return lax.ppermute(block, axes, route)


def vmem(n):
    return [pl.BlockSpec(memory_space=pltpu.VMEM)] * n


def vmem(n):
    return [pl.BlockSpec(memory_space=pltpu.VMEM)] * n


def anywhere(n):
    return [pl.BlockSpec(memory_space=pl.ANY)] * n


def body(mode_shapes, stress_field, displacement, material, fixed_nodes, eigenvalues, mode_weight):
    nx, ny, nz = material.shape
    dims = (nx, ny)
    width = nx + 3
    sds = jax.ShapeDtypeStruct
    tile = (MODES, LANES)
    layer = 6 * ny + ny // 2
    tiles, x1, x2, edge, ex1, ex2 = pl.pallas_call(
        functools.partial(pack_kernel, dims),
        out_shape=(
            sds((GROUPS, nx, ny) + tile, BF16),
            sds((layer,) + tile, BF16),
            sds((layer,) + tile, BF16),
            sds((GROUPS,) + tile, BF16),
            sds((GROUPS,) + tile, BF16),
            sds((GROUPS,) + tile, BF16),
        ),
        in_specs=anywhere(4),
        out_specs=tuple(vmem(6)),
        scratch_shapes=[
            pltpu.VMEM(mode_shapes.shape, BF16),
            pltpu.VMEM(material.shape, material.dtype),
            pltpu.VMEM(fixed_nodes.shape, fixed_nodes.dtype),
            pltpu.VMEM(displacement.shape, F32),
            pltpu.VMEM((GROUPS * MODES * PITCH, LANES), F32),
            pltpu.SemaphoreType.DMA((6,)),
        ],
        compiler_params=pltpu.CompilerParams(vmem_limit_bytes=8 << 20),
        name="pack",
    )(*(pltpu.with_memory_space_constraint(a, pltpu.HBM) for a in (mode_shapes, material, fixed_nodes, displacement)))

    xz = ("gx", "gz")
    zkinds = (1,) if lax.axis_size("gz") == 2 else (1, 2)
    r2 = swap(x2, xz, (2, 0), True)
    r1 = swap(x1, xz, (1, 0), True)
    rz = [swap(edge, xz, (0, k), True) for k in zkinds]
    rz1 = [swap(ex1, xz, (1, k), True) for k in zkinds]
    rz2 = [swap(ex2, xz, (2, k), True) for k in zkinds]
    count = 6 * width + (nx + 2) // 2 + GROUPS
    rim, y1, y2 = pl.pallas_call(
        functools.partial(merge_kernel, dims, len(zkinds)),
        out_shape=(sds((GROUPS, width) + tile, F32), sds((count,) + tile, BF16), sds((count,) + tile, BF16)),
        in_specs=vmem(3 + 3 * len(zkinds)),
        out_specs=tuple(vmem(3)),
        scratch_shapes=[pltpu.VMEM((nx + 2, HALF, LANES), F32)],
        compiler_params=pltpu.CompilerParams(vmem_limit_bytes=8 << 20),
        name="merge",
    )(tiles, r1, r2, *rz, *rz1, *rz2)

    yz = ("gy", "gz")
    ry1 = swap(y1, yz, (1, 0), True)
    ry2 = swap(y2, yz, (2, 0), True)
    sens, wmain, field, cell, zr, scale = pl.pallas_call(
        functools.partial(inner_kernel, dims),
        out_shape=(
            sds((MODES * nx * ny, LANES), F32),
            sds((6, nx + 2, 8, LANES), F32),
            sds((FIELDS, nx + 2, ny, LANES), F32),
            sds((7, nx, ny, LANES), F32),
            sds((GROUPS, width) + tile, F32),
            sds((3,) + tile, F32),
        ),
        in_specs=vmem(5) + [pl.BlockSpec(memory_space=pltpu.SMEM)] * 2,
        out_specs=tuple(vmem(6)),
        scratch_shapes=[
            pltpu.VMEM((3, width, ny) + tile, BF16),
            pltpu.VMEM((ny, 3, width) + tile, F32),
            pltpu.VMEM((ny, 3, width) + tile, F32),
            pltpu.VMEM((6, ny - 1, 8, LANES), F32),
            pltpu.VMEM(((nx + 2) * ny * HALF, LANES), F32),
        ],
        compiler_params=pltpu.CompilerParams(vmem_limit_bytes=24 << 20),
        cost_estimate=pl.CostEstimate(flops=20_000_000, bytes_accessed=12_000_000, transcendentals=0),
        name="inner",
    )(tiles, r1, r2, rim, stress_field, eigenvalues, mode_weight)
    sens, adjoint = pl.pallas_call(
        functools.partial(final_kernel, dims),
        out_shape=(sds((MODES, nx, ny, LANES), F32), sds((nx, ny, LANES), F32)),
        in_specs=vmem(10) + anywhere(1),
        out_specs=(pl.BlockSpec(memory_space=pl.ANY), pl.BlockSpec(memory_space=pltpu.VMEM)),
        input_output_aliases={10: 0},
        scratch_shapes=[
            pltpu.VMEM((5, 3 * width) + tile, BF16),
            pltpu.VMEM((2, (nx + 2) // 2) + tile, F32),
            pltpu.VMEM((2, GROUPS) + tile, F32),
            pltpu.VMEM((5, 3, width) + tile, F32),
            pltpu.VMEM((5, 3, width) + tile, F32),
            pltpu.VMEM((6, 3, 8, LANES), F32),
            pltpu.VMEM((6, nx + 2, 16, 2 * LANES), F32),
            pltpu.VMEM((GROUPS, LANES, LANES), F32),
            pltpu.VMEM((FIELDS, nx + 2, 24, LANES), F32),
            pltpu.VMEM((8, 2, 24, LANES), F32),
            pltpu.VMEM((6, nx + 1, 2, 16, LANES), F32),
            pltpu.VMEM((2, 24, LANES), F32),
            pltpu.VMEM((nx,) + tile, F32),
            pltpu.SemaphoreType.DMA((nx,)),
        ],
        compiler_params=pltpu.CompilerParams(vmem_limit_bytes=24 << 20),
        name="finish",
    )(y1, y2, ry1, ry2, rim, wmain, field, cell, zr, scale, sens.reshape(MODES, nx, ny, nz))
    return sens, adjoint


def solution(mesh):
    return jax.shard_map(
        body,
        mesh=mesh,
        in_specs=(
            P(None, None, "gx", "gy", "gz"),
            P(None, "gx", "gy", "gz"),
            P(None, "gx", "gy", "gz"),
            P("gx", "gy", "gz"),
            P("gx", "gy", "gz"),
            P(),
            P(),
        ),
        out_specs=(P(None, "gx", "gy", "gz"), P("gx", "gy", "gz")),
        check_vma=False,
    )
```

```python
import functools
import math

import jax
import jax.numpy as jnp
from jax import lax
from jax.experimental import pallas as pl
from jax.experimental.pallas import tpu as pltpu
from jax.sharding import PartitionSpec as P

LEVELS = 8
POISSON = 0.45
LAM = POISSON / ((1.0 + POISSON) * (1.0 - 2.0 * POISSON))
MU = 0.5 / (1.0 + POISSON)
R3 = 1.0 / math.sqrt(3.0)
F32 = jnp.float32
BF16 = jnp.bfloat16
MODES = 16
GROUPS = 4
LANES = 128


def lane_iota(shape=(MODES, LANES)):
    return lax.broadcasted_iota(jnp.int32, shape, len(shape) - 1)


def row_iota(shape):
    return lax.broadcasted_iota(jnp.int32, shape, 0)


def roll(value, shift, axis=1):
    size = value.shape[axis]
    if isinstance(shift, int):
        shift = shift % size
        if shift == 0:
            return value
    return pltpu.roll(value, shift, axis)


def place(axis):
    me = lax.axis_index(axis)
    size = lax.axis_size(axis)
    even = lax.rem(me, 2) == 0
    return even, me > 0, me < size - 1


HALF = 8
PITCH = 33


def pair_up(first, second):
    return jnp.concatenate([first[:HALF].astype(F32), second[:HALF].astype(F32)], 0).astype(BF16)


def pack_kernel(dims, modes_in, material_in, fixed_in, disp_in, tiles, x1, x2, edge, ex1, ex2, modes, material, fixed, disp, raw, chosen, sems):
    nx, ny = dims
    copies = [
        pltpu.make_async_copy(src, dst, sems.at[i])
        for i, (src, dst) in enumerate(
            [(modes_in.at[c], modes.at[c]) for c in range(3)]
            + [(material_in, material), (fixed_in, fixed), (disp_in, disp)]
        )
    ]
    for copy in copies:
        copy.start()
    part = nx * ny
    col = lane_iota((LANES, LANES))
    kind = lax.rem(col, 3)
    wanted = jnp.where(row_iota((LANES, LANES)) == jnp.where(kind == 0, LANES - 1, kind - 1), 1.0, 0.0)
    for y in range(ny):
        table = jnp.where((col >= 3 * y) & (col < 3 * y + 3), wanted, 0.0)
        chosen[y * LANES : (y + 1) * LANES, :] = table.astype(BF16)

    def store(c, m, value):
        start = (c * MODES + m) * PITCH
        raw[start : start + part, :] = value.reshape(part, LANES)

    def spread(c):
        @pl.loop(0, nx)
        def _(x):
            for y in range(ny):
                value = raw[pl.ds(c * MODES * PITCH + x * ny + y, MODES, stride=PITCH), :]
                tiles[c, x, y] = value.astype(BF16)

    for c in range(3):
        copies[c].wait()
        for m in range(MODES):
            store(c, m, modes[c, m].astype(F32))
        spread(c)
    for copy in copies[3:]:
        copy.wait()
    store(3, 0, material[...].astype(F32) + 1.0)
    store(3, 1, 1.0 - fixed[...].astype(F32))
    for c in range(3):
        value = disp[c]
        first = value.astype(BF16).astype(F32)
        store(3, 2 + c, first)
        store(3, 5 + c, value - first)
    for m in range(HALF, MODES):
        store(3, m, jnp.zeros((part, LANES), F32))
    spread(3)

    block = jnp.concatenate([tiles[:, :, y].reshape(GROUPS * nx * MODES, LANES) for y in range(ny)], 1)
    ends = jnp.dot(block, chosen[...], preferred_element_type=F32)
    ends = ends.reshape(GROUPS, nx, MODES, LANES)
    pieces = LANES // nx
    even, _, _ = place("gx")
    last = [ends[c, nx - 1] for c in range(GROUPS)]
    for c in range(GROUPS):
        total = ends[c, 0]
        for x in range(1, nx):
            total = total + roll(ends[c, x], pieces * x)
        edge[c] = total.astype(BF16)
    for out, out_edge, upward in ((x1, ex1, even), (x2, ex2, jnp.logical_not(even))):
        flag = upward.astype(F32)
        for s in range(2):
            layer = jnp.where(upward, nx - 1, s)
            for c in range(3):
                for y in range(ny):
                    out[(c * 2 + s) * ny + y] = tiles[c, layer, y]
        layer = jnp.where(upward, nx - 1, 0)
        for y in range(0, ny, 2):
            out[6 * ny + y // 2] = pair_up(tiles[3, layer, y], tiles[3, layer, y + 1])
        for c in range(GROUPS):
            below = ends[c, 0] + roll(ends[c, 1], pieces)
            out_edge[c] = (last[c] * flag + below * (1.0 - flag)).astype(BF16)


def pick(parity, lower, upper, first, second, use_lower, use_upper, none_lower, none_upper):
    odd = jnp.logical_not(parity)
    pl.when(jnp.logical_and(lower, parity))(lambda: use_lower(second))
    pl.when(jnp.logical_and(lower, odd))(lambda: use_lower(first))
    pl.when(jnp.logical_and(upper, parity))(lambda: use_upper(first))
    pl.when(jnp.logical_and(upper, odd))(lambda: use_upper(second))
    pl.when(jnp.logical_not(lower))(none_lower)
    pl.when(jnp.logical_not(upper))(none_upper)


def z_partners(zcount):
    even, lower, upper = place("gz")
    lower, upper = lower.astype(F32), upper.astype(F32)
    if zcount == 1:
        return [(lower, upper)]
    even = even.astype(F32)
    return [(lower * (1.0 - even), upper * even), (lower * even, upper * (1.0 - even))]


def merge_kernel(dims, zcount, *refs):
    nx, ny = dims
    rz2 = refs[:zcount]
    rz1 = refs[zcount : 2 * zcount]
    rz = refs[2 * zcount : 3 * zcount]
    r2, r1, tiles = refs[3 * zcount : 3 + 3 * zcount]
    y1, y2, rows_aux, ends_here = refs[3 + 3 * zcount :]
    xe, xlo, xup = place("gx")
    ye, _, _ = place("gy")
    width = nx + 3
    pieces = LANES // nx
    sides = z_partners(zcount)
    row = row_iota((LANES, LANES))
    col = lane_iota((LANES, LANES))
    turn = lax.rem(row, pieces)
    slot = row // pieces
    end = lax.rem(col, 16)
    layer = col // 16
    usable = (turn < 3 * ny) & (end < 6)
    low_side = jnp.where(usable & (lax.rem(turn, 3) == 0), 1.0, 0.0)
    high_side = jnp.where(usable & (lax.rem(turn, 3) != 0), 1.0, 0.0)

    blank = jnp.zeros((MODES, LANES), BF16)
    blank_half = jnp.zeros((HALF, LANES), F32)

    def half_of(ref, row):
        pairs = ref[6 * ny + row // 2].astype(F32)
        odd = lax.rem(row, 2).astype(F32)
        return pairs[:HALF] * (1.0 - odd) + pairs[HALF:] * odd

    for out, upward in ((y1, ye), (y2, jnp.logical_not(ye))):
        rows = [jnp.where(upward, ny - 1, s) for s in range(2)]
        for c in range(3):
            for s in range(2):
                for x in range(nx):
                    out[(c * width + x + 1) * 2 + s] = tiles[c, x, rows[s]]
        for x in range(nx):
            rows_aux[x + 1] = tiles[3, x, rows[0]][:HALF].astype(F32)

        def lower(ref, out=out, rows=rows):
            for c in range(3):
                for s in range(2):
                    out[c * width * 2 + s] = ref[c * 2 * ny + rows[s]]
            rows_aux[0] = half_of(ref, rows[0])

        def upper(ref, out=out, rows=rows):
            for c in range(3):
                for t in range(2):
                    for s in range(2):
                        out[(c * width + nx + 1 + t) * 2 + s] = ref[(c * 2 + t) * ny + rows[s]]
            rows_aux[nx + 1] = half_of(ref, rows[0])

        def no_lower(out=out):
            for c in range(3):
                for s in range(2):
                    out[c * width * 2 + s] = blank
            rows_aux[0] = blank_half

        def no_upper(out=out):
            for c in range(3):
                for i in range(4):
                    out[(c * width + nx + 1) * 2 + i] = blank
            rows_aux[nx + 1] = blank_half

        pick(xe, xlo, xup, r1, r2, lower, upper, no_lower, no_upper)
        base = 6 * width
        for x in range(0, nx + 2, 2):
            out[base + x // 2] = jnp.concatenate([rows_aux[x], rows_aux[x + 1]], 0).astype(BF16)
        base += (nx + 2) // 2
        match = turn == end + 3 * rows[0]
        tables = [jnp.where(match, low_side * lo + high_side * up, 0.0) for lo, up in sides]

        def chosen(refs, offset, count):
            total = None
            for ref, table in zip(refs, tables, strict=True):
                wanted = jnp.where((layer == slot + offset) & (slot < count), table, 0.0).astype(BF16)
                block = ref[...].reshape(GROUPS * MODES, LANES)
                term = jnp.dot(block, wanted, preferred_element_type=F32)
                total = term if total is None else total + term
            return total

        ends_here[...] = chosen(rz, 1, nx)

        def add_lower(refs, chosen=chosen):
            ends_here[...] += chosen(refs, 0, 1)

        def add_upper(refs, chosen=chosen):
            ends_here[...] += chosen(refs, nx + 1, 2)

        def nothing():
            pass

        pick(xe, xlo, xup, rz1, rz2, add_lower, add_upper, nothing, nothing)
        out[base : base + GROUPS] = ends_here[...].reshape(GROUPS, MODES, LANES).astype(BF16)


def cross_xy(a, b):
    return a[0] * b[1] + a[4] * b[5]


def cross_xz(a, b):
    return a[0] * b[2] + a[3] * b[5]


def cross_yz(a, b):
    return a[1] * b[2] + a[3] * b[4]


def squares(a):
    f, g, h, t = a[3] * a[3], a[4] * a[4], a[5] * a[5], a[6] * a[6]
    ft = f + t
    return (a[0] * a[0] + (ft + g), a[1] * a[1] + (ft + h), a[2] * a[2] + ((g + t) + h))


def combos(now, after):
    return (
        now[1] + after[1],
        after[0] - now[0],
        now[2] + after[2],
        (after[1] - now[1]) * R3,
        (now[3] + after[3]) * R3,
        (after[2] - now[2]) * R3,
        (after[3] - now[3]) * (1.0 / 3.0),
    )


def forms(parts, with_energy):
    own = [squares(p) for p in parts]
    quad = [own[0][i] + own[1][i] + own[2][i] for i in range(3)]
    for f in (cross_yz, cross_xz, cross_xy):
        quad.append(f(parts[0], parts[0]) + f(parts[1], parts[1]) + f(parts[2], parts[2]))
    if not with_energy:
        return quad, None
    x, y, z = parts
    energy = (
        MU * (quad[0] + quad[1] + quad[2])
        + (LAM + MU) * (own[0][0] + own[1][1] + own[2][2])
        + (2.0 * LAM) * (cross_xy(x, y) + cross_xz(x, z) + cross_yz(y, z))
        + (2.0 * MU) * (cross_xy(y, x) + cross_xz(z, x) + cross_yz(z, y))
    )
    return quad, energy


def bilinear(l, d):
    total = None
    diagonal = None
    for p in range(3):
        prod = [l[p][i] * d[p][i] for i in range(7)]
        ft = prod[3] + prod[6]
        three = (
            prod[0] + (ft + prod[4]),
            prod[1] + (ft + prod[5]),
            prod[2] + ((prod[4] + prod[6]) + prod[5]),
        )
        whole = three[0] + three[1] + three[2]
        total = whole if total is None else total + whole
        diagonal = three[p] if diagonal is None else diagonal + three[p]
    lx, ly, lz = l
    dx, dy, dz = d
    mixed = (
        (cross_xy(lx, dy) + cross_xy(dx, ly))
        + (cross_xz(lx, dz) + cross_xz(dx, lz))
        + (cross_yz(ly, dz) + cross_yz(dy, lz))
    )
    shear = (
        (cross_xy(dy, lx) + cross_xy(ly, dx))
        + (cross_xz(dz, lx) + cross_xz(lz, dx))
        + (cross_yz(dz, ly) + cross_yz(lz, dy))
    )
    return MU * total + (LAM + MU) * diagonal + LAM * mixed + MU * shear


def fold_rows(values):
    row = row_iota((8, LANES))
    top = row < 4
    step = [
        jnp.where(top, values[k], values[k + 4]) + roll(jnp.where(top, values[k + 4], values[k]), 4, 0)
        for k in range(4)
    ]
    top = lax.rem(row, 4) < 2
    step = [
        jnp.where(top, step[k] + roll(step[k], 6, 0), step[k + 2] + roll(step[k + 2], 2, 0)) for k in range(2)
    ]
    return jnp.where(lax.rem(row, 2) == 0, step[0] + roll(step[0], 7, 0), step[1] + roll(step[1], 1, 0))


def z_table():
    row = row_iota((LANES, 2 * LANES))
    col = lane_iota((LANES, 2 * LANES))
    z = jnp.where(col < LANES, col, col - LANES)
    own = jnp.where(row == z, jnp.where(col < LANES, 1.0, -1.0), 0.0)
    return (own + jnp.where(row == z + 1, 1.0, 0.0)).astype(BF16)


def rim_table(kind):
    row = row_iota((LANES, 2 * LANES))
    z = lax.rem(lane_iota((LANES, 2 * LANES)), LANES)
    return jnp.where((z == LANES - 1) & (row == kind), 1.0, 0.0).astype(BF16)


def first_column(lane_to):
    return jnp.where((row_iota((LANES, LANES)) == 0) & (lane_iota((LANES, LANES)) == lane_to), 1.0, 0.0).astype(BF16)


def rows_along_z(block, rim, kind, table, sz, dz, at):
    table[LANES:, :] = rim_table(kind)
    both = jnp.dot(jnp.concatenate([block, rim], 1), table[...], preferred_element_type=F32)
    sz[at] = both[:, :LANES].reshape(sz.shape[1:])
    dz[at] = both[:, LANES:].reshape(dz.shape[1:])


def x_parts(sz, dz, y, x, h):
    found = []
    for c in range(3):
        s0 = sz[y, c, x, pl.ds(8 * h, 8), :]
        s1 = sz[y, c, x + 1, pl.ds(8 * h, 8), :]
        d0 = dz[y, c, x, pl.ds(8 * h, 8), :]
        d1 = dz[y, c, x + 1, pl.ds(8 * h, 8), :]
        found.append((s0 + s1, s1 - s0, d0 + d1, d1 - d0))
    return found


def mode_value(quad, energy, fields, eig_rows):
    terms = [fields[i] * quad[i] for i in range(6)]
    total = ((terms[0] + terms[1]) + (terms[2] + terms[3])) + (terms[4] + terms[5])
    return fields[6] * energy + eig_rows * total


FIELDS = 5


def inner_kernel(dims, zcount, *refs):
    rz = refs[:zcount]
    rz1 = refs[zcount : 2 * zcount]
    rz2 = refs[2 * zcount : 3 * zcount]
    tiles, r1, r2, stress, eig, weight = refs[3 * zcount : 3 * zcount + 6]
    sens, wmain, field, cell, zr, scale, rim, full, sz, dz, part, aux, table = refs[3 * zcount + 6 :]
    nx, ny = dims
    width = nx + 3
    tall = ny + 3
    lane = lane_iota()
    xe, xlo, xup = place("gx")
    table[0:LANES, :] = z_table()

    pieces = LANES // nx
    sides = z_partners(zcount)
    low_lane = (lane < 3 * ny) & (lax.rem(lane, 3) == 0)
    high_lane = (lane < 3 * ny) & (lax.rem(lane, 3) != 0)

    def merged(blocks, slot):
        total = None
        for block, (lo, up) in zip(blocks, sides, strict=True):
            mask = jnp.where(low_lane, lo, 0.0) + jnp.where(high_lane, up, 0.0)
            term = roll(block.astype(F32), LANES - pieces * slot) * mask
            total = term if total is None else total + term
        return total

    for c in range(GROUPS):
        for x in range(nx):
            rim[c, x + 1] = merged([r[c] for r in rz], x)

    def rim_lower(refs):
        for c in range(GROUPS):
            rim[c, 0] = merged([r[c] for r in refs], 0)

    def rim_upper(refs):
        for c in range(GROUPS):
            for s in range(2):
                rim[c, nx + 1 + s] = merged([r[c] for r in refs], s)

    def rim_no_lower():
        rim[:, 0] = jnp.zeros((GROUPS, MODES, LANES), F32)

    def rim_no_upper():
        rim[:, nx + 1 : nx + 3] = jnp.zeros((GROUPS, 2, MODES, LANES), F32)

    pick(xe, xlo, xup, rz1, rz2, rim_lower, rim_upper, rim_no_lower, rim_no_upper)

    full[:, 1 : nx + 1] = tiles[0:3]
    for x in range(nx):
        for y in range(ny):
            aux[((x + 1) * ny + y) * HALF : ((x + 1) * ny + y + 1) * HALF, :] = tiles[3, x, y][:HALF].astype(F32)

    def halves(ref, x):
        for i in range(ny // 2):
            start = (x * ny + 2 * i) * HALF
            aux[start : start + 2 * HALF, :] = ref[6 * ny + i].astype(F32)

    def lower(ref):
        for c in range(3):
            for y in range(ny):
                full[c, 0, y] = ref[c * 2 * ny + y]
        halves(ref, 0)

    def upper(ref):
        for c in range(3):
            for s in range(2):
                for y in range(ny):
                    full[c, nx + 1 + s, y] = ref[(c * 2 + s) * ny + y]
        halves(ref, nx + 1)

    def no_lower():
        full[:, 0:1] = jnp.zeros((3, 1, ny, MODES, LANES), BF16)
        aux[0 : ny * HALF, :] = jnp.zeros((ny * HALF, LANES), F32)

    def no_upper():
        full[:, nx + 1 : nx + 3] = jnp.zeros((3, 2, ny, MODES, LANES), BF16)
        aux[(nx + 1) * ny * HALF : (nx + 2) * ny * HALF, :] = jnp.zeros((ny * HALF, LANES), F32)

    pick(xe, xlo, xup, r1, r2, lower, upper, no_lower, no_upper)

    count = 3 * width * MODES
    ends = rim[0:3].reshape(count, LANES).astype(BF16)
    column = None
    for y in range(ny):
        block = full[:, :, y].reshape(count, LANES)
        rows_along_z(block, ends, 3 * y + 1, table, sz, dz, y)
        term = jnp.dot(block, first_column(3 * tall + y + 1), preferred_element_type=F32)
        column = term if column is None else column + term
    column = column.reshape(3, width, MODES, LANES)
    for c in range(GROUPS):
        for x in range(width):
            turned = roll(rim[c, x], 3)
            zr[c, x] = turned + column[c, x] if c < 3 else turned

    for x in range(nx + 2):
        def channel(k):
            return aux[pl.ds(x * ny * HALF + k, ny, stride=HALF), :]

        field[0, x] = channel(0)
        field[1, x] = channel(1)
        for c in range(3):
            field[2 + c, x] = channel(2 + c) + channel(5 + c)

    mode_row = row_iota((MODES, LANES))
    mode_lane = lax.rem(lane, MODES)
    eig_rows = jnp.zeros((MODES, LANES), F32)
    coef_rows = jnp.zeros((MODES, LANES), F32)
    coef_lanes = jnp.zeros((MODES, LANES), F32)
    for m in range(MODES):
        product = eig[m] * weight[m]
        eig_rows = jnp.where(mode_row == m, eig[m], eig_rows)
        coef_rows = jnp.where(mode_row == m, product, coef_rows)
        coef_lanes = jnp.where(mode_lane == m, product, coef_lanes)
    scale[0], scale[1], scale[2] = eig_rows, coef_rows, coef_lanes

    for x in range(nx):
        density = field[0, x + 1] * (1.0 / LEVELS)
        young = 0.001 + density * density * density
        slope = 3.0 * density * density
        ratio = slope / young
        cell[6, x] = slope * (1.0 / 16.0)
        for c in range(6):
            cell[c, x] = stress[c, x] * ratio * (-1.0 / 16.0 if c < 3 else -1.0 / 8.0)

    def sweep(x, inside):
        for h in range(2):
            coef = scale[1, 8 * h : 8 * h + 8]
            eig_half = scale[0, 8 * h : 8 * h + 8]
            now = x_parts(sz, dz, 0, x, h)
            for y in range(ny - 1):
                after = x_parts(sz, dz, y + 1, x, h)
                quad, energy = forms([combos(now[c], after[c]) for c in range(3)], inside)
                if inside:
                    fields = [cell[i, x - 1, pl.ds(y, 1), :] for i in range(7)]
                    start = 8 * h * nx * ny + (x - 1) * ny + y
                    sens[pl.ds(start, 8, stride=nx * ny), :] = mode_value(quad, energy, fields, eig_half)
                for i in range(6):
                    if h == 0:
                        part[i, y] = coef * quad[i]
                    else:
                        part[i, y] += coef * quad[i]
                now = after
        blank = jnp.zeros((8, LANES), F32)
        for i in range(6):
            wmain[i, x] = fold_rows([blank] + [part[i, y] for y in range(ny - 1)])

    @pl.loop(1, nx + 1)
    def _(x):
        sweep(x, True)

    @pl.loop(0, 2)
    def _(i):
        sweep(i * (nx + 1), False)


def final_kernel(dims, y1, y2, r1, r2, wmain, field_in, cell, zr, scale, sens_in, sens, adjoint, rows, rows_aux, rows_end, sz, dz, sum_z, w, zt, field, shear, load, stage, whole, table, sem):
    nx, ny = dims
    width = nx + 3
    tall = ny + 3
    lane = lane_iota()
    ye, ylo, yup = place("gy")
    table[0:LANES, :] = z_table()
    whole[...] = sens_in[...]

    def copy_rows(to, ref, slot):
        for i in range(3 * width):
            rows[to, i] = ref[2 * i + slot]

    aux_base = 6 * width
    end_base = aux_base + (nx + 2) // 2

    def copy_aux(to, ref):
        for i in range((nx + 2) // 2):
            rows_aux[to, i] = ref[aux_base + i].astype(F32)
        for c in range(GROUPS):
            rows_end[to, c] = ref[end_base + c].astype(F32)

    def lower(ref):
        copy_rows(0, ref, 0)
        copy_aux(0, ref)

    def upper(ref):
        copy_rows(3, ref, 0)
        copy_rows(4, ref, 1)
        copy_aux(1, ref)

    def no_lower():
        rows[0] = jnp.zeros_like(rows[0])
        rows_aux[0] = jnp.zeros_like(rows_aux[0])
        rows_end[0] = jnp.zeros_like(rows_end[0])

    def no_upper():
        rows[3:5] = jnp.zeros_like(rows[3:5])
        rows_aux[1] = jnp.zeros_like(rows_aux[1])
        rows_end[1] = jnp.zeros_like(rows_end[1])

    pick(ye, ylo, yup, r1, r2, lower, upper, no_lower, no_upper)

    @pl.when(ye)
    def _():
        copy_rows(2, y1, 0)
        copy_rows(1, y2, 0)

    @pl.when(jnp.logical_not(ye))
    def _():
        copy_rows(2, y2, 0)
        copy_rows(1, y1, 0)

    far = 3 * (ny + 1)
    count = 3 * width * MODES
    at = (0, 1, ny, ny + 1, ny + 2)
    column = None
    for i in (0, 3, 4):
        term = jnp.dot(rows[i].reshape(count, LANES), first_column(3 * tall + at[i]), preferred_element_type=F32)
        column = term if column is None else column + term
    column = column.reshape(3, width, MODES, LANES)
    full_rim = []
    for c in range(GROUPS):
        layers = []
        for x in range(width):
            ends = jnp.where(lane < 3, roll(rows_end[0, c], LANES - 16 * x), zr[c, x])
            ends = jnp.where((lane >= far) & (lane < far + 6), roll(rows_end[1, c], far - 16 * x), ends)
            if c < 3:
                ends = ends + column[c, x]
            layers.append(ends)
        layers.append(jnp.zeros((LANES - width * MODES, LANES), F32))
        stacked = jnp.concatenate(layers, 0)
        full_rim.append(stacked[: width * MODES])
        zt[c] = stacked.T
    ends = jnp.concatenate(full_rim[:3], 0).astype(BF16)
    for i in range(5):
        rows_along_z(rows[i].reshape(count, LANES), ends, 3 * at[i] + 1, table, sz, dz, i)

    w[:, :, 0:8, 0:LANES] = wmain[...]

    def sweep(x, inside):
        for h in range(2):
            coef = scale[1, 8 * h : 8 * h + 8]
            now = None
            for i, (first, own) in enumerate(((0, False), (2, inside), (3, False))):
                if i < 2:
                    now = x_parts(sz, dz, first, x, h)
                after = x_parts(sz, dz, first + 1, x, h)
                quad, energy = forms([combos(now[c], after[c]) for c in range(3)], own)
                if own:
                    fields = [cell[k, x - 1, ny - 1 : ny, :] for k in range(7)]
                    start = 8 * h * nx * ny + x * ny - 1
                    value = mode_value(quad, energy, fields, scale[0, 8 * h : 8 * h + 8])
                    whole[pl.ds(start, 8, stride=nx * ny), :] = value
                for k in range(6):
                    if h == 0:
                        sum_z[k, i] = coef * quad[k]
                    else:
                        sum_z[k, i] += coef * quad[k]
                now = after
        pairs = [(k, i) for k in range(6) for i in range(3)]
        for start in range(0, len(pairs), 8):
            some = pairs[start : start + 8]
            values = [sum_z[k, i] for k, i in some]
            values += [jnp.zeros((8, LANES), F32)] * (8 - len(some))
            folded = fold_rows(values)
            for j, (k, i) in enumerate(some):
                row = (0, ny, ny + 1)[i]
                w[k, x, row : row + 1, 0:LANES] = folded[j : j + 1]

    @pl.loop(1, nx + 1)
    def _(x):
        sweep(x, True)

    @pl.loop(0, 2)
    def _(i):
        sweep(i * (nx + 1), False)

    copy = pltpu.make_async_copy(whole, sens, sem)
    copy.start()

    for x in range(nx + 2):
        for k in range(FIELDS):
            field[k, x, 1 : ny + 1] = field_in[k, x]
        for side, row in ((0, 0), (1, ny + 1)):
            pair = rows_aux[side, x // 2][(x % 2) * HALF : (x % 2 + 1) * HALF]
            field[0, x, row : row + 1] = pair[0:1]
            field[1, x, row : row + 1] = pair[1:2]
            for c in range(3):
                field[2 + c, x, row : row + 1] = pair[2 + c : 3 + c] + pair[5 + c : 6 + c]

    def end_nodes(c, kind, y):
        if kind == 3:
            return zt[c, pl.ds(3 * tall + y, 16), :]
        return zt[c, pl.ds(3 * y + kind, 16, stride=3), :]

    def end_parts(low, high, y):
        found = []
        for c in range(3):
            first, second = end_nodes(c, low, y), end_nodes(c, high, y)
            s, d = first + second, second - first
            s_next, d_next = roll(s, LANES - 16), roll(d, LANES - 16)
            found.append((s + s_next, s_next - s, d + d_next, d_next - d))
        return found

    sides = []
    for low, high in ((0, 3), (1, 2)):
        now, after = end_parts(low, high, 0), end_parts(low, high, 1)
        quad, _ = forms([combos(now[c], after[c]) for c in range(3)], False)
        sides.append([value * scale[2] for value in quad])

    def narrow(first, second, shift):
        kept = lax.rem(lane, 2 * shift) < shift
        return jnp.where(kept, first + roll(first, LANES - shift), second + roll(second, shift))

    step = [narrow(sides[0][i], sides[1][i], 1) for i in range(6)]
    step = [narrow(step[i], step[i + 1], 2) for i in (0, 2, 4)]
    step = [narrow(step[0], step[1], 4), step[2] + roll(step[2], LANES - 4)]
    packed = narrow(step[0], step[1], 8)
    for i in range(6):
        for x in range(nx + 2):
            w[i, x, 0:16, LANES:] = roll(packed, LANES - (16 * x + 2 * i + 1))

    def end_field(channel, x, first, with_low):
        value = roll(zt[3, pl.ds(3 * first + 1, 16, stride=3), :], LANES - (16 * x + channel))
        if not with_low:
            return value
        low = roll(zt[3, pl.ds(3 * first, 16, stride=3), :], LANES - 1 - (16 * x + channel))
        return jnp.where(lane == 0, value, jnp.where(lane == LANES - 1, low, 0.0))

    def z_back(main, end):
        turned, turned_end = roll(main, 1), roll(end, 1)
        return jnp.where(lane == 0, turned_end, turned), jnp.where(lane == 0, turned, turned_end)

    first_rows = None
    for x in range(nx + 2):
        level = (field[0, x, 0:16], end_field(0, x, 0, True))
        scaled = []
        for t in range(2):
            density = level[t] * (1.0 / LEVELS)
            young = 0.001 + density * density * density
            young = jnp.where(level[t] > 0.0, young, 0.0) * (1.0 / 64.0)
            value = [w[i, x, 0:16, LANES * t : LANES * (t + 1)] * young for i in range(6)]
            trace = LAM * (value[0] + value[1] + value[2])
            scaled.append(
                [trace + (2.0 * MU) * value[i] for i in range(3)] + [(2.0 * MU) * value[i] for i in range(3, 6)]
            )
        sums, diffs = [], []
        for i in range(6):
            main, end = scaled[0][i], scaled[1][i]
            back_main, back_end = z_back(main, end)
            sums.append((main + back_main, end + back_end))
            diffs.append((main - back_main, end - back_end))
        xx, yy, zz, yz, xz, xy = range(6)
        order = (sums[xx], sums[xy], diffs[xz], sums[yy], diffs[yz], sums[xz], sums[yz], diffs[zz])
        for slot, source in enumerate(order):
            for t in range(2):
                shear[slot, t, 0:16] = source[t]
        found = []
        for t in range(2):
            low = [shear[slot, t, 0:16] for slot in range(8)]
            high = [shear[slot, t, 1:17] for slot in range(8)]
            plus = [low[k] + high[k] for k in range(8)]
            minus = [high[k] - low[k] for k in range(8)]
            found.append([plus[0], minus[1] + plus[2], plus[1], minus[3] + plus[4], plus[5], minus[6] + plus[7]])
        if x > 0:
            node = x - 1
            for t in range(2):
                free = field[1, x, 1:17] if t == 0 else end_field(1, x, 1, False)
                for p in range(3):
                    value = (found[t][2 * p] - first_rows[t][2 * p]) + (
                        found[t][2 * p + 1] + first_rows[t][2 * p + 1]
                    )
                    load[p, node, t] = value * free
                    if t == 0:
                        shift = field[2 + p, x, 1:17]
                    else:
                        shift = end_field(2 + p, x, 1, False) + end_field(5 + p, x, 1, False)
                    load[3 + p, node, t] = shift
        first_rows = found

    def node_layer(x):
        found = []
        for f in range(6):
            main, end = load[f, x, 0], load[f, x, 1]
            after = jnp.where(lane == LANES - 1, roll(end, LANES - 1), roll(main, LANES - 1))
            s, d = main + after, after - main
            stage[0, 0:16] = s
            stage[1, 0:16] = d
            s_next, d_next = stage[0, 1:9], stage[1, 1:9]
            s, d = s[0:8], d[0:8]
            found.append((s + s_next, s_next - s, d + d_next, d_next - d))
        return found

    def layer_combos(now, after):
        return (
            after[0] - now[0],
            now[1] + after[1],
            now[2] + after[2],
            (after[1] - now[1]) * R3,
            (after[2] - now[2]) * R3,
            (now[3] + after[3]) * R3,
            (after[3] - now[3]) * (1.0 / 3.0),
        )

    now = node_layer(0)
    for x in range(nx):
        after = node_layer(x + 1)
        parts = [layer_combos(now[f], after[f]) for f in range(6)]
        adjoint[x] = cell[6, x] * bilinear(parts[:3], parts[3:])
        now = after
    copy.wait()


def partner(index, size, kind):
    other = index ^ 1 if kind == 1 else ((index + 1) ^ 1) - 1
    return other if 0 <= other < size else None


def swap(block, axes, kinds, fill):
    sizes = [lax.axis_size(a) for a in axes]
    route = []
    for i in range(sizes[0]):
        for j in range(sizes[1]):
            ends = [p if k == 0 else partner(p, n, k) for p, n, k in zip((i, j), sizes, kinds, strict=True)]
            if ends[0] is None:
                ends = [i, partner(j, sizes[1], 1)] if fill else None
            elif ends[1] is None:
                ends = [partner(i, sizes[0], 1) if kinds[0] == 0 else ends[0], j] if fill else None
            if ends is not None:
                route.append((i * sizes[1] + j, ends[0] * sizes[1] + ends[1]))
    return lax.ppermute(block, axes, route)


def vmem(n):
    return [pl.BlockSpec(memory_space=pltpu.VMEM)] * n


def vmem(n):
    return [pl.BlockSpec(memory_space=pltpu.VMEM)] * n


def anywhere(n):
    return [pl.BlockSpec(memory_space=pl.ANY)] * n


def body(mode_shapes, stress_field, displacement, material, fixed_nodes, eigenvalues, mode_weight):
    nx, ny, nz = material.shape
    dims = (nx, ny)
    width = nx + 3
    sds = jax.ShapeDtypeStruct
    tile = (MODES, LANES)
    layer = 6 * ny + ny // 2
    tiles, x1, x2, edge, ex1, ex2 = pl.pallas_call(
        functools.partial(pack_kernel, dims),
        out_shape=(
            sds((GROUPS, nx, ny) + tile, BF16),
            sds((layer,) + tile, BF16),
            sds((layer,) + tile, BF16),
            sds((GROUPS,) + tile, BF16),
            sds((GROUPS,) + tile, BF16),
            sds((GROUPS,) + tile, BF16),
        ),
        in_specs=anywhere(4),
        out_specs=tuple(vmem(6)),
        scratch_shapes=[
            pltpu.VMEM(mode_shapes.shape, BF16),
            pltpu.VMEM(material.shape, material.dtype),
            pltpu.VMEM(fixed_nodes.shape, fixed_nodes.dtype),
            pltpu.VMEM(displacement.shape, F32),
            pltpu.VMEM((GROUPS * MODES * PITCH, LANES), F32),
            pltpu.VMEM((ny * LANES, LANES), BF16),
            pltpu.SemaphoreType.DMA((6,)),
        ],
        compiler_params=pltpu.CompilerParams(vmem_limit_bytes=8 << 20),
        name="pack",
    )(*(pltpu.with_memory_space_constraint(a, pltpu.HBM) for a in (mode_shapes, material, fixed_nodes, displacement)))

    xz = ("gx", "gz")
    zkinds = (1,) if lax.axis_size("gz") == 2 else (1, 2)
    r2 = swap(x2, xz, (2, 0), True)
    r1 = swap(x1, xz, (1, 0), True)
    rz = [swap(edge, xz, (0, k), True) for k in zkinds]
    rz1 = [swap(ex1, xz, (1, k), True) for k in zkinds]
    rz2 = [swap(ex2, xz, (2, k), True) for k in zkinds]
    count = 6 * width + (nx + 2) // 2 + GROUPS
    y1, y2 = pl.pallas_call(
        functools.partial(merge_kernel, dims, len(zkinds)),
        out_shape=(sds((count,) + tile, BF16), sds((count,) + tile, BF16)),
        in_specs=vmem(3 + 3 * len(zkinds)),
        out_specs=tuple(vmem(2)),
        scratch_shapes=[pltpu.VMEM((nx + 2, HALF, LANES), F32), pltpu.VMEM((GROUPS * MODES, LANES), F32)],
        compiler_params=pltpu.CompilerParams(vmem_limit_bytes=8 << 20),
        name="merge",
    )(*rz2, *rz1, *rz, r2, r1, tiles)

    yz = ("gy", "gz")
    ry1 = swap(y1, yz, (1, 0), True)
    ry2 = swap(y2, ("gx", "gy"), (0, 2), True)
    sens, wmain, field, cell, zr, scale = pl.pallas_call(
        functools.partial(inner_kernel, dims, len(zkinds)),
        out_shape=(
            sds((MODES * nx * ny, LANES), F32),
            sds((6, nx + 2, 8, LANES), F32),
            sds((FIELDS, nx + 2, ny, LANES), F32),
            sds((7, nx, ny, LANES), F32),
            sds((GROUPS, width) + tile, F32),
            sds((3,) + tile, F32),
        ),
        in_specs=vmem(4 + 3 * len(zkinds)) + [pl.BlockSpec(memory_space=pltpu.SMEM)] * 2,
        out_specs=tuple(vmem(6)),
        scratch_shapes=[
            pltpu.VMEM((GROUPS, width) + tile, F32),
            pltpu.VMEM((3, width, ny) + tile, BF16),
            pltpu.VMEM((ny, 3, width) + tile, F32),
            pltpu.VMEM((ny, 3, width) + tile, F32),
            pltpu.VMEM((6, ny - 1, 8, LANES), F32),
            pltpu.VMEM(((nx + 2) * ny * HALF, LANES), F32),
            pltpu.VMEM((2 * LANES, 2 * LANES), BF16),
        ],
        compiler_params=pltpu.CompilerParams(vmem_limit_bytes=24 << 20),
        cost_estimate=pl.CostEstimate(flops=20_000_000, bytes_accessed=12_000_000, transcendentals=0),
        name="inner",
    )(*rz, *rz1, *rz2, tiles, r1, r2, stress_field, eigenvalues, mode_weight)
    sens, adjoint = pl.pallas_call(
        functools.partial(final_kernel, dims),
        out_shape=(sds((MODES * nx * ny, LANES), F32), sds((nx, ny, LANES), F32)),
        in_specs=vmem(10),
        out_specs=(pl.BlockSpec(memory_space=pl.ANY), pl.BlockSpec(memory_space=pltpu.VMEM)),
        scratch_shapes=[
            pltpu.VMEM((5, 3 * width) + tile, BF16),
            pltpu.VMEM((2, (nx + 2) // 2) + tile, F32),
            pltpu.VMEM((2, GROUPS) + tile, F32),
            pltpu.VMEM((5, 3, width) + tile, F32),
            pltpu.VMEM((5, 3, width) + tile, F32),
            pltpu.VMEM((6, 3, 8, LANES), F32),
            pltpu.VMEM((6, nx + 2, 16, 2 * LANES), F32),
            pltpu.VMEM((GROUPS, LANES, LANES), F32),
            pltpu.VMEM((FIELDS, nx + 2, 24, LANES), F32),
            pltpu.VMEM((8, 2, 24, LANES), F32),
            pltpu.VMEM((6, nx + 1, 2, 16, LANES), F32),
            pltpu.VMEM((2, 24, LANES), F32),
            pltpu.VMEM((MODES * nx * ny, LANES), F32),
            pltpu.VMEM((2 * LANES, 2 * LANES), BF16),
            pltpu.SemaphoreType.DMA,
        ],
        compiler_params=pltpu.CompilerParams(vmem_limit_bytes=24 << 20),
        name="finish",
    )(y1, y2, ry1, ry2, wmain, field, cell, zr, scale, sens)
    return sens.reshape(MODES, nx, ny, nz), adjoint


def solution(mesh):
    return jax.shard_map(
        body,
        mesh=mesh,
        in_specs=(
            P(None, None, "gx", "gy", "gz"),
            P(None, "gx", "gy", "gz"),
            P(None, "gx", "gy", "gz"),
            P("gx", "gy", "gz"),
            P("gx", "gy", "gz"),
            P(),
            P(),
        ),
        out_specs=(P(None, "gx", "gy", "gz"), P("gx", "gy", "gz")),
        check_vma=False,
    )
```

```python
import functools
import math

import jax
import jax.numpy as jnp
from jax import lax
from jax.experimental import pallas as pl
from jax.experimental.pallas import tpu as pltpu
from jax.sharding import PartitionSpec as P

LEVELS = 8
POISSON = 0.45
LAM = POISSON / ((1.0 + POISSON) * (1.0 - 2.0 * POISSON))
MU = 0.5 / (1.0 + POISSON)
R3 = 1.0 / math.sqrt(3.0)
F32 = jnp.float32
BF16 = jnp.bfloat16
MODES = 16
GROUPS = 4
LANES = 128


def lane_iota(shape=(MODES, LANES)):
    return lax.broadcasted_iota(jnp.int32, shape, len(shape) - 1)


def row_iota(shape):
    return lax.broadcasted_iota(jnp.int32, shape, 0)


def roll(value, shift, axis=1):
    size = value.shape[axis]
    if isinstance(shift, int):
        shift = shift % size
        if shift == 0:
            return value
    return pltpu.roll(value, shift, axis)


def place(axis):
    me = lax.axis_index(axis)
    size = lax.axis_size(axis)
    even = lax.rem(me, 2) == 0
    return even, me > 0, me < size - 1


HALF = 8
PITCH = 33


def pair_up(first, second):
    return jnp.concatenate([first[:HALF].astype(F32), second[:HALF].astype(F32)], 0).astype(BF16)


def pack_kernel(dims, zcount, modes_in, material_in, fixed_in, disp_in, tiles, x1, x2, edge, ex1, ex2, tables, modes, material, fixed, disp, raw, chosen, sems):
    nx, ny = dims
    copies = [
        pltpu.make_async_copy(src, dst, sems.at[i])
        for i, (src, dst) in enumerate(
            [(modes_in.at[c], modes.at[c]) for c in range(3)]
            + [(material_in, material), (fixed_in, fixed), (disp_in, disp)]
        )
    ]
    for copy in copies:
        copy.start()
    part = nx * ny
    col = lane_iota((LANES, LANES))
    kind = lax.rem(col, 3)
    wanted = jnp.where(row_iota((LANES, LANES)) == jnp.where(kind == 0, LANES - 1, kind - 1), 1.0, 0.0)
    for y in range(ny):
        table = jnp.where((col >= 3 * y) & (col < 3 * y + 3), wanted, 0.0)
        chosen[y * LANES : (y + 1) * LANES, :] = table.astype(BF16)

    def store_table(index, table):
        tables[index * LANES : (index + 1) * LANES, :] = table

    rim_tables(dims, zcount, store_table)

    def store(c, m, value):
        start = (c * MODES + m) * PITCH
        raw[start : start + part, :] = value.reshape(part, LANES)

    def spread(c):
        @pl.loop(0, nx)
        def _(x):
            for y in range(ny):
                value = raw[pl.ds(c * MODES * PITCH + x * ny + y, MODES, stride=PITCH), :]
                tiles[c, x, y] = value.astype(BF16)

    for c in range(3):
        copies[c].wait()
        for m in range(MODES):
            store(c, m, modes[c, m].astype(F32))
        spread(c)
    for copy in copies[3:]:
        copy.wait()
    store(3, 0, material[...].astype(F32) + 1.0)
    store(3, 1, 1.0 - fixed[...].astype(F32))
    for c in range(3):
        value = disp[c]
        first = value.astype(BF16).astype(F32)
        store(3, 2 + c, first)
        store(3, 5 + c, value - first)
    for m in range(HALF, MODES):
        store(3, m, jnp.zeros((part, LANES), F32))
    spread(3)

    block = jnp.concatenate([tiles[:, :, y].reshape(GROUPS * nx * MODES, LANES) for y in range(ny)], 1)
    ends = jnp.dot(block, chosen[...], preferred_element_type=F32)
    ends = ends.reshape(GROUPS, nx, MODES, LANES)
    pieces = LANES // nx
    even, _, _ = place("gx")
    last = [ends[c, nx - 1] for c in range(GROUPS)]
    for c in range(GROUPS):
        total = ends[c, 0]
        for x in range(1, nx):
            total = total + roll(ends[c, x], pieces * x)
        edge[c] = total.astype(BF16)
    for out, out_edge, upward in ((x1, ex1, even), (x2, ex2, jnp.logical_not(even))):
        flag = upward.astype(F32)
        for s in range(2):
            layer = jnp.where(upward, nx - 1, s)
            for c in range(3):
                for y in range(ny):
                    out[(c * 2 + s) * ny + y] = tiles[c, layer, y]
        layer = jnp.where(upward, nx - 1, 0)
        for y in range(0, ny, 2):
            out[6 * ny + y // 2] = pair_up(tiles[3, layer, y], tiles[3, layer, y + 1])
        for c in range(GROUPS):
            below = ends[c, 0] + roll(ends[c, 1], pieces)
            out_edge[c] = (last[c] * flag + below * (1.0 - flag)).astype(BF16)


def pick(parity, lower, upper, first, second, use_lower, use_upper, none_lower, none_upper):
    odd = jnp.logical_not(parity)
    pl.when(jnp.logical_and(lower, parity))(lambda: use_lower(second))
    pl.when(jnp.logical_and(lower, odd))(lambda: use_lower(first))
    pl.when(jnp.logical_and(upper, parity))(lambda: use_upper(first))
    pl.when(jnp.logical_and(upper, odd))(lambda: use_upper(second))
    pl.when(jnp.logical_not(lower))(none_lower)
    pl.when(jnp.logical_not(upper))(none_upper)


def z_partners(zcount):
    even, lower, upper = place("gz")
    lower, upper = lower.astype(F32), upper.astype(F32)
    if zcount == 1:
        return [(lower, upper)]
    even = even.astype(F32)
    return [(lower * (1.0 - even), upper * even), (lower * even, upper * (1.0 - even))]


def z_partners(zcount):
    even, lower, upper = place("gz")
    lower, upper = lower.astype(F32), upper.astype(F32)
    if zcount == 1:
        return [(lower, upper)]
    even = even.astype(F32)
    return [(lower * (1.0 - even), upper * even), (lower * even, upper * (1.0 - even))]


def rim_tables(dims, zcount, store):
    nx, ny = dims
    pieces = LANES // nx
    xe, xlo, xup = place("gx")
    ye, _, _ = place("gy")
    xe, xlo, xup = xe.astype(F32), xlo.astype(F32), xup.astype(F32)
    row = row_iota((LANES, 2 * LANES))
    col = lane_iota((LANES, 2 * LANES))
    second = col >= LANES
    col = lax.rem(col, LANES)
    turn = lax.rem(row, pieces)
    slot = row // pieces
    end = lax.rem(col, 16)
    layer = col // 16
    last = jnp.where(ye, 3 * ny - 3, 0)
    first_row = jnp.where(second, 3 * ny - 3 - last, last)
    fits = (turn == end + first_row) & (turn < 3 * ny) & (end < 6)
    low = lax.rem(turn, 3) == 0
    own = jnp.where(layer == slot + 1, 1.0, 0.0)
    below = jnp.where((layer == 0) & (slot == 0), xlo, 0.0)
    above = jnp.where((layer == slot + nx + 1) & (slot < 2), xup, 0.0)
    by_kind = (below * xe + above * (1.0 - xe), above * xe + below * (1.0 - xe), own)
    for z, (lower, upper) in enumerate(z_partners(zcount)):
        valid = jnp.where(fits, jnp.where(low, lower, upper), 0.0)
        for k, kind in enumerate(by_kind):
            store(k * zcount + z, (valid * kind).astype(BF16))


def merge_kernel(dims, zcount, *refs):
    nx, ny = dims
    zblocks = refs[: 3 * zcount]
    r2, r1, tiles, tables, y1, y2, rows_aux = refs[3 * zcount :]
    xe, xlo, xup = place("gx")
    ye, _, _ = place("gy")
    width = nx + 3
    side = jnp.concatenate([ref[...].reshape(GROUPS * MODES, LANES) for ref in zblocks], 1)
    ends = jnp.dot(side, tables[...], preferred_element_type=F32)
    rows = [[jnp.where(up, ny - 1, s) for s in range(2)] for up in (ye, jnp.logical_not(ye))]
    outs = (y1, y2)
    blank = jnp.zeros((MODES, LANES), BF16)
    blank_half = jnp.zeros((HALF, LANES), F32)

    def half_of(ref, row):
        pairs = ref[6 * ny + row // 2].astype(F32)
        odd = lax.rem(row, 2).astype(F32)
        return pairs[:HALF] * (1.0 - odd) + pairs[HALF:] * odd

    def lower(ref):
        for k in range(2):
            for c in range(3):
                for s in range(2):
                    outs[k][c * width * 2 + s] = ref[c * 2 * ny + rows[k][s]]
            rows_aux[k, 0] = half_of(ref, rows[k][0])

    def upper(ref):
        for k in range(2):
            for c in range(3):
                for t in range(2):
                    for s in range(2):
                        outs[k][(c * width + nx + 1 + t) * 2 + s] = ref[(c * 2 + t) * ny + rows[k][s]]
            rows_aux[k, nx + 1] = half_of(ref, rows[k][0])

    def no_lower():
        for k in range(2):
            for c in range(3):
                for s in range(2):
                    outs[k][c * width * 2 + s] = blank
            rows_aux[k, 0] = blank_half

    def no_upper():
        for k in range(2):
            for c in range(3):
                for i in range(4):
                    outs[k][(c * width + nx + 1) * 2 + i] = blank
            rows_aux[k, nx + 1] = blank_half

    pick(xe, xlo, xup, r1, r2, lower, upper, no_lower, no_upper)
    base = 6 * width
    for k, out in enumerate(outs):
        for c in range(3):
            for s in range(2):
                for x in range(nx):
                    out[(c * width + x + 1) * 2 + s] = tiles[c, x, rows[k][s]]
        for x in range(nx):
            rows_aux[k, x + 1] = tiles[3, x, rows[k][0]][:HALF].astype(F32)
        for x in range(0, nx + 2, 2):
            out[base + x // 2] = pair_up(rows_aux[k, x], rows_aux[k, x + 1])
        block = ends[:, k * LANES : (k + 1) * LANES].reshape(GROUPS, MODES, LANES)
        out[base + (nx + 2) // 2 :] = block.astype(BF16)


def cross_xy(a, b):
    return a[0] * b[1] + a[4] * b[5]


def cross_xz(a, b):
    return a[0] * b[2] + a[3] * b[5]


def cross_yz(a, b):
    return a[1] * b[2] + a[3] * b[4]


def squares(a):
    f, g, h, t = a[3] * a[3], a[4] * a[4], a[5] * a[5], a[6] * a[6]
    ft = f + t
    return (a[0] * a[0] + (ft + g), a[1] * a[1] + (ft + h), a[2] * a[2] + ((g + t) + h))


def combos(now, after):
    return (
        now[1] + after[1],
        after[0] - now[0],
        now[2] + after[2],
        (after[1] - now[1]) * R3,
        (now[3] + after[3]) * R3,
        (after[2] - now[2]) * R3,
        (after[3] - now[3]) * (1.0 / 3.0),
    )


def forms(parts, with_energy):
    own = [squares(p) for p in parts]
    quad = [own[0][i] + own[1][i] + own[2][i] for i in range(3)]
    for f in (cross_yz, cross_xz, cross_xy):
        quad.append(f(parts[0], parts[0]) + f(parts[1], parts[1]) + f(parts[2], parts[2]))
    if not with_energy:
        return quad, None
    x, y, z = parts
    energy = (
        MU * (quad[0] + quad[1] + quad[2])
        + (LAM + MU) * (own[0][0] + own[1][1] + own[2][2])
        + (2.0 * LAM) * (cross_xy(x, y) + cross_xz(x, z) + cross_yz(y, z))
        + (2.0 * MU) * (cross_xy(y, x) + cross_xz(z, x) + cross_yz(z, y))
    )
    return quad, energy


def bilinear(l, d):
    total = None
    diagonal = None
    for p in range(3):
        prod = [l[p][i] * d[p][i] for i in range(7)]
        ft = prod[3] + prod[6]
        three = (
            prod[0] + (ft + prod[4]),
            prod[1] + (ft + prod[5]),
            prod[2] + ((prod[4] + prod[6]) + prod[5]),
        )
        whole = three[0] + three[1] + three[2]
        total = whole if total is None else total + whole
        diagonal = three[p] if diagonal is None else diagonal + three[p]
    lx, ly, lz = l
    dx, dy, dz = d
    mixed = (
        (cross_xy(lx, dy) + cross_xy(dx, ly))
        + (cross_xz(lx, dz) + cross_xz(dx, lz))
        + (cross_yz(ly, dz) + cross_yz(dy, lz))
    )
    shear = (
        (cross_xy(dy, lx) + cross_xy(ly, dx))
        + (cross_xz(dz, lx) + cross_xz(lz, dx))
        + (cross_yz(dz, ly) + cross_yz(lz, dy))
    )
    return MU * total + (LAM + MU) * diagonal + LAM * mixed + MU * shear


def fold_rows(values):
    row = row_iota((8, LANES))
    top = row < 4
    step = [
        jnp.where(top, values[k], values[k + 4]) + roll(jnp.where(top, values[k + 4], values[k]), 4, 0)
        for k in range(4)
    ]
    top = lax.rem(row, 4) < 2
    step = [
        jnp.where(top, step[k] + roll(step[k], 6, 0), step[k + 2] + roll(step[k + 2], 2, 0)) for k in range(2)
    ]
    return jnp.where(lax.rem(row, 2) == 0, step[0] + roll(step[0], 7, 0), step[1] + roll(step[1], 1, 0))


def z_table():
    row = row_iota((LANES, 2 * LANES))
    col = lane_iota((LANES, 2 * LANES))
    z = jnp.where(col < LANES, col, col - LANES)
    own = jnp.where(row == z, jnp.where(col < LANES, 1.0, -1.0), 0.0)
    return (own + jnp.where(row == z + 1, 1.0, 0.0)).astype(BF16)


def rim_table(kind):
    row = row_iota((LANES, 2 * LANES))
    z = lax.rem(lane_iota((LANES, 2 * LANES)), LANES)
    return jnp.where((z == LANES - 1) & (row == kind), 1.0, 0.0).astype(BF16)


def first_column(lane_to):
    return jnp.where((row_iota((LANES, LANES)) == 0) & (lane_iota((LANES, LANES)) == lane_to), 1.0, 0.0).astype(BF16)


def rows_along_z(block, rim, kind, table, sz, dz, at):
    table[LANES:, :] = rim_table(kind)
    both = jnp.dot(jnp.concatenate([block, rim], 1), table[...], preferred_element_type=F32)
    sz[at] = both[:, :LANES].reshape(sz.shape[1:])
    dz[at] = both[:, LANES:].reshape(dz.shape[1:])


def x_parts(sz, dz, y, x, h):
    found = []
    for c in range(3):
        s0 = sz[y, c, x, pl.ds(8 * h, 8), :]
        s1 = sz[y, c, x + 1, pl.ds(8 * h, 8), :]
        d0 = dz[y, c, x, pl.ds(8 * h, 8), :]
        d1 = dz[y, c, x + 1, pl.ds(8 * h, 8), :]
        found.append((s0 + s1, s1 - s0, d0 + d1, d1 - d0))
    return found


def mode_value(quad, energy, fields, eig_rows):
    terms = [fields[i] * quad[i] for i in range(6)]
    total = ((terms[0] + terms[1]) + (terms[2] + terms[3])) + (terms[4] + terms[5])
    return fields[6] * energy + eig_rows * total


FIELDS = 5


def inner_kernel(dims, zcount, *refs):
    rz = refs[:zcount]
    rz1 = refs[zcount : 2 * zcount]
    rz2 = refs[2 * zcount : 3 * zcount]
    tiles, r1, r2, stress, eig, weight = refs[3 * zcount : 3 * zcount + 6]
    sens, wmain, field, cell, zr, scale, rim, full, sz, dz, part, aux, table = refs[3 * zcount + 6 :]
    nx, ny = dims
    width = nx + 3
    tall = ny + 3
    lane = lane_iota()
    xe, xlo, xup = place("gx")
    table[0:LANES, :] = z_table()

    pieces = LANES // nx
    sides = z_partners(zcount)
    low_lane = (lane < 3 * ny) & (lax.rem(lane, 3) == 0)
    high_lane = (lane < 3 * ny) & (lax.rem(lane, 3) != 0)

    def merged(blocks, slot):
        total = None
        for block, (lo, up) in zip(blocks, sides, strict=True):
            mask = jnp.where(low_lane, lo, 0.0) + jnp.where(high_lane, up, 0.0)
            term = roll(block.astype(F32), LANES - pieces * slot) * mask
            total = term if total is None else total + term
        return total

    for c in range(GROUPS):
        for x in range(nx):
            rim[c, x + 1] = merged([r[c] for r in rz], x)

    def rim_lower(refs):
        for c in range(GROUPS):
            rim[c, 0] = merged([r[c] for r in refs], 0)

    def rim_upper(refs):
        for c in range(GROUPS):
            for s in range(2):
                rim[c, nx + 1 + s] = merged([r[c] for r in refs], s)

    def rim_no_lower():
        rim[:, 0] = jnp.zeros((GROUPS, MODES, LANES), F32)

    def rim_no_upper():
        rim[:, nx + 1 : nx + 3] = jnp.zeros((GROUPS, 2, MODES, LANES), F32)

    pick(xe, xlo, xup, rz1, rz2, rim_lower, rim_upper, rim_no_lower, rim_no_upper)

    full[:, 1 : nx + 1] = tiles[0:3]
    for x in range(nx):
        for y in range(ny):
            aux[((x + 1) * ny + y) * HALF : ((x + 1) * ny + y + 1) * HALF, :] = tiles[3, x, y][:HALF].astype(F32)

    def halves(ref, x):
        for i in range(ny // 2):
            start = (x * ny + 2 * i) * HALF
            aux[start : start + 2 * HALF, :] = ref[6 * ny + i].astype(F32)

    def lower(ref):
        for c in range(3):
            for y in range(ny):
                full[c, 0, y] = ref[c * 2 * ny + y]
        halves(ref, 0)

    def upper(ref):
        for c in range(3):
            for s in range(2):
                for y in range(ny):
                    full[c, nx + 1 + s, y] = ref[(c * 2 + s) * ny + y]
        halves(ref, nx + 1)

    def no_lower():
        full[:, 0:1] = jnp.zeros((3, 1, ny, MODES, LANES), BF16)
        aux[0 : ny * HALF, :] = jnp.zeros((ny * HALF, LANES), F32)

    def no_upper():
        full[:, nx + 1 : nx + 3] = jnp.zeros((3, 2, ny, MODES, LANES), BF16)
        aux[(nx + 1) * ny * HALF : (nx + 2) * ny * HALF, :] = jnp.zeros((ny * HALF, LANES), F32)

    pick(xe, xlo, xup, r1, r2, lower, upper, no_lower, no_upper)

    count = 3 * width * MODES
    ends = rim[0:3].reshape(count, LANES).astype(BF16)
    column = None
    for y in range(ny):
        block = full[:, :, y].reshape(count, LANES)
        rows_along_z(block, ends, 3 * y + 1, table, sz, dz, y)
        term = jnp.dot(block, first_column(3 * tall + y + 1), preferred_element_type=F32)
        column = term if column is None else column + term
    column = column.reshape(3, width, MODES, LANES)
    for c in range(GROUPS):
        for x in range(width):
            turned = roll(rim[c, x], 3)
            zr[c, x] = turned + column[c, x] if c < 3 else turned

    for x in range(nx + 2):
        def channel(k):
            return aux[pl.ds(x * ny * HALF + k, ny, stride=HALF), :]

        field[0, x] = channel(0)
        field[1, x] = channel(1)
        for c in range(3):
            field[2 + c, x] = channel(2 + c) + channel(5 + c)

    mode_row = row_iota((MODES, LANES))
    mode_lane = lax.rem(lane, MODES)
    eig_rows = jnp.zeros((MODES, LANES), F32)
    coef_rows = jnp.zeros((MODES, LANES), F32)
    coef_lanes = jnp.zeros((MODES, LANES), F32)
    for m in range(MODES):
        product = eig[m] * weight[m]
        eig_rows = jnp.where(mode_row == m, eig[m], eig_rows)
        coef_rows = jnp.where(mode_row == m, product, coef_rows)
        coef_lanes = jnp.where(mode_lane == m, product, coef_lanes)
    scale[0], scale[1], scale[2] = eig_rows, coef_rows, coef_lanes

    for x in range(nx):
        density = field[0, x + 1] * (1.0 / LEVELS)
        young = 0.001 + density * density * density
        slope = 3.0 * density * density
        ratio = slope / young
        cell[6, x] = slope * (1.0 / 16.0)
        for c in range(6):
            cell[c, x] = stress[c, x] * ratio * (-1.0 / 16.0 if c < 3 else -1.0 / 8.0)

    def sweep(x, inside):
        for h in range(2):
            coef = scale[1, 8 * h : 8 * h + 8]
            eig_half = scale[0, 8 * h : 8 * h + 8]
            now = x_parts(sz, dz, 0, x, h)
            for y in range(ny - 1):
                after = x_parts(sz, dz, y + 1, x, h)
                quad, energy = forms([combos(now[c], after[c]) for c in range(3)], inside)
                if inside:
                    fields = [cell[i, x - 1, pl.ds(y, 1), :] for i in range(7)]
                    start = 8 * h * nx * ny + (x - 1) * ny + y
                    sens[pl.ds(start, 8, stride=nx * ny), :] = mode_value(quad, energy, fields, eig_half)
                for i in range(6):
                    if h == 0:
                        part[x, i, y] = coef * quad[i]
                    else:
                        part[x, i, y] += coef * quad[i]
                now = after
        blank = jnp.zeros((8, LANES), F32)
        for i in range(6):
            wmain[i, x] = fold_rows([blank] + [part[x, i, y] for y in range(ny - 1)])

    for x in range(1, nx + 1):
        sweep(x, True)
    for x in (0, nx + 1):
        sweep(x, False)


def final_kernel(dims, y1, y2, r1, r2, wmain, field_in, cell, zr, scale, sens_in, sens, adjoint, rows, rows_aux, rows_end, sz, dz, sum_z, w, zt, field, shear, load, stage, whole, table, sem):
    nx, ny = dims
    width = nx + 3
    tall = ny + 3
    lane = lane_iota()
    ye, ylo, yup = place("gy")
    table[0:LANES, :] = z_table()
    whole[...] = sens_in[...]

    def copy_rows(to, ref, slot):
        for i in range(3 * width):
            rows[to, i] = ref[2 * i + slot]

    aux_base = 6 * width
    end_base = aux_base + (nx + 2) // 2

    def copy_aux(to, ref):
        for i in range((nx + 2) // 2):
            rows_aux[to, i] = ref[aux_base + i].astype(F32)
        for c in range(GROUPS):
            rows_end[to, c] = ref[end_base + c].astype(F32)

    def lower(ref):
        copy_rows(0, ref, 0)
        copy_aux(0, ref)

    def upper(ref):
        copy_rows(3, ref, 0)
        copy_rows(4, ref, 1)
        copy_aux(1, ref)

    def no_lower():
        rows[0] = jnp.zeros_like(rows[0])
        rows_aux[0] = jnp.zeros_like(rows_aux[0])
        rows_end[0] = jnp.zeros_like(rows_end[0])

    def no_upper():
        rows[3:5] = jnp.zeros_like(rows[3:5])
        rows_aux[1] = jnp.zeros_like(rows_aux[1])
        rows_end[1] = jnp.zeros_like(rows_end[1])

    pick(ye, ylo, yup, r1, r2, lower, upper, no_lower, no_upper)

    @pl.when(ye)
    def _():
        copy_rows(2, y1, 0)
        copy_rows(1, y2, 0)

    @pl.when(jnp.logical_not(ye))
    def _():
        copy_rows(2, y2, 0)
        copy_rows(1, y1, 0)

    far = 3 * (ny + 1)
    count = 3 * width * MODES
    at = (0, 1, ny, ny + 1, ny + 2)
    column = None
    for i in (0, 3, 4):
        term = jnp.dot(rows[i].reshape(count, LANES), first_column(3 * tall + at[i]), preferred_element_type=F32)
        column = term if column is None else column + term
    column = column.reshape(3, width, MODES, LANES)
    full_rim = []
    for c in range(GROUPS):
        layers = []
        for x in range(width):
            ends = jnp.where(lane < 3, roll(rows_end[0, c], LANES - 16 * x), zr[c, x])
            ends = jnp.where((lane >= far) & (lane < far + 6), roll(rows_end[1, c], far - 16 * x), ends)
            if c < 3:
                ends = ends + column[c, x]
            layers.append(ends)
        layers.append(jnp.zeros((LANES - width * MODES, LANES), F32))
        stacked = jnp.concatenate(layers, 0)
        full_rim.append(stacked[: width * MODES])
        zt[c] = stacked.T
    ends = jnp.concatenate(full_rim[:3], 0).astype(BF16)
    for i in range(5):
        rows_along_z(rows[i].reshape(count, LANES), ends, 3 * at[i] + 1, table, sz, dz, i)

    w[:, :, 0:8, 0:LANES] = wmain[...]

    def sweep(x, inside):
        for h in range(2):
            coef = scale[1, 8 * h : 8 * h + 8]
            now = None
            for i, (first, own) in enumerate(((0, False), (2, inside), (3, False))):
                if i < 2:
                    now = x_parts(sz, dz, first, x, h)
                after = x_parts(sz, dz, first + 1, x, h)
                quad, energy = forms([combos(now[c], after[c]) for c in range(3)], own)
                if own:
                    fields = [cell[k, x - 1, ny - 1 : ny, :] for k in range(7)]
                    start = 8 * h * nx * ny + x * ny - 1
                    value = mode_value(quad, energy, fields, scale[0, 8 * h : 8 * h + 8])
                    whole[pl.ds(start, 8, stride=nx * ny), :] = value
                for k in range(6):
                    if h == 0:
                        sum_z[k, i] = coef * quad[k]
                    else:
                        sum_z[k, i] += coef * quad[k]
                now = after
        pairs = [(k, i) for k in range(6) for i in range(3)]
        for start in range(0, len(pairs), 8):
            some = pairs[start : start + 8]
            values = [sum_z[k, i] for k, i in some]
            values += [jnp.zeros((8, LANES), F32)] * (8 - len(some))
            folded = fold_rows(values)
            for j, (k, i) in enumerate(some):
                row = (0, ny, ny + 1)[i]
                w[k, x, row : row + 1, 0:LANES] = folded[j : j + 1]

    for x in range(1, nx + 1):
        sweep(x, True)
    for x in (0, nx + 1):
        sweep(x, False)

    copy = pltpu.make_async_copy(whole, sens, sem)
    copy.start()

    for x in range(nx + 2):
        for k in range(FIELDS):
            field[k, x, 1 : ny + 1] = field_in[k, x]
        for side, row in ((0, 0), (1, ny + 1)):
            pair = rows_aux[side, x // 2][(x % 2) * HALF : (x % 2 + 1) * HALF]
            field[0, x, row : row + 1] = pair[0:1]
            field[1, x, row : row + 1] = pair[1:2]
            for c in range(3):
                field[2 + c, x, row : row + 1] = pair[2 + c : 3 + c] + pair[5 + c : 6 + c]

    def end_nodes(c, kind, y):
        if kind == 3:
            return zt[c, pl.ds(3 * tall + y, 16), :]
        return zt[c, pl.ds(3 * y + kind, 16, stride=3), :]

    def end_parts(low, high, y):
        found = []
        for c in range(3):
            first, second = end_nodes(c, low, y), end_nodes(c, high, y)
            s, d = first + second, second - first
            s_next, d_next = roll(s, LANES - 16), roll(d, LANES - 16)
            found.append((s + s_next, s_next - s, d + d_next, d_next - d))
        return found

    sides = []
    for low, high in ((0, 3), (1, 2)):
        now, after = end_parts(low, high, 0), end_parts(low, high, 1)
        quad, _ = forms([combos(now[c], after[c]) for c in range(3)], False)
        sides.append([value * scale[2] for value in quad])

    def narrow(first, second, shift):
        kept = lax.rem(lane, 2 * shift) < shift
        return jnp.where(kept, first + roll(first, LANES - shift), second + roll(second, shift))

    step = [narrow(sides[0][i], sides[1][i], 1) for i in range(6)]
    step = [narrow(step[i], step[i + 1], 2) for i in (0, 2, 4)]
    step = [narrow(step[0], step[1], 4), step[2] + roll(step[2], LANES - 4)]
    packed = narrow(step[0], step[1], 8)
    for i in range(6):
        for x in range(nx + 2):
            w[i, x, 0:16, LANES:] = roll(packed, LANES - (16 * x + 2 * i + 1))

    def end_field(channel, x, first, with_low):
        value = roll(zt[3, pl.ds(3 * first + 1, 16, stride=3), :], LANES - (16 * x + channel))
        if not with_low:
            return value
        low = roll(zt[3, pl.ds(3 * first, 16, stride=3), :], LANES - 1 - (16 * x + channel))
        return jnp.where(lane == 0, value, jnp.where(lane == LANES - 1, low, 0.0))

    def z_back(main, end):
        turned, turned_end = roll(main, 1), roll(end, 1)
        return jnp.where(lane == 0, turned_end, turned), jnp.where(lane == 0, turned, turned_end)

    first_rows = None
    for x in range(nx + 2):
        level = (field[0, x, 0:16], end_field(0, x, 0, True))
        scaled = []
        for t in range(2):
            density = level[t] * (1.0 / LEVELS)
            young = 0.001 + density * density * density
            young = jnp.where(level[t] > 0.0, young, 0.0) * (1.0 / 64.0)
            value = [w[i, x, 0:16, LANES * t : LANES * (t + 1)] * young for i in range(6)]
            trace = LAM * (value[0] + value[1] + value[2])
            scaled.append(
                [trace + (2.0 * MU) * value[i] for i in range(3)] + [(2.0 * MU) * value[i] for i in range(3, 6)]
            )
        sums, diffs = [], []
        for i in range(6):
            main, end = scaled[0][i], scaled[1][i]
            back_main, back_end = z_back(main, end)
            sums.append((main + back_main, end + back_end))
            diffs.append((main - back_main, end - back_end))
        xx, yy, zz, yz, xz, xy = range(6)
        order = (sums[xx], sums[xy], diffs[xz], sums[yy], diffs[yz], sums[xz], sums[yz], diffs[zz])
        for slot, source in enumerate(order):
            for t in range(2):
                shear[slot, t, 0:16] = source[t]
        found = []
        for t in range(2):
            low = [shear[slot, t, 0:16] for slot in range(8)]
            high = [shear[slot, t, 1:17] for slot in range(8)]
            plus = [low[k] + high[k] for k in range(8)]
            minus = [high[k] - low[k] for k in range(8)]
            found.append([plus[0], minus[1] + plus[2], plus[1], minus[3] + plus[4], plus[5], minus[6] + plus[7]])
        if x > 0:
            node = x - 1
            for t in range(2):
                free = field[1, x, 1:17] if t == 0 else end_field(1, x, 1, False)
                for p in range(3):
                    value = (found[t][2 * p] - first_rows[t][2 * p]) + (
                        found[t][2 * p + 1] + first_rows[t][2 * p + 1]
                    )
                    load[p, node, t] = value * free
                    if t == 0:
                        shift = field[2 + p, x, 1:17]
                    else:
                        shift = end_field(2 + p, x, 1, False) + end_field(5 + p, x, 1, False)
                    load[3 + p, node, t] = shift
        first_rows = found

    def node_layer(x):
        found = []
        for f in range(6):
            main, end = load[f, x, 0], load[f, x, 1]
            after = jnp.where(lane == LANES - 1, roll(end, LANES - 1), roll(main, LANES - 1))
            s, d = main + after, after - main
            stage[0, 0:16] = s
            stage[1, 0:16] = d
            s_next, d_next = stage[0, 1:9], stage[1, 1:9]
            s, d = s[0:8], d[0:8]
            found.append((s + s_next, s_next - s, d + d_next, d_next - d))
        return found

    def layer_combos(now, after):
        return (
            after[0] - now[0],
            now[1] + after[1],
            now[2] + after[2],
            (after[1] - now[1]) * R3,
            (after[2] - now[2]) * R3,
            (now[3] + after[3]) * R3,
            (after[3] - now[3]) * (1.0 / 3.0),
        )

    now = node_layer(0)
    for x in range(nx):
        after = node_layer(x + 1)
        parts = [layer_combos(now[f], after[f]) for f in range(6)]
        adjoint[x] = cell[6, x] * bilinear(parts[:3], parts[3:])
        now = after
    copy.wait()


def partner(index, size, kind):
    other = index ^ 1 if kind == 1 else ((index + 1) ^ 1) - 1
    return other if 0 <= other < size else None


def swap(block, axes, kinds, fill):
    sizes = [lax.axis_size(a) for a in axes]
    route = []
    for i in range(sizes[0]):
        for j in range(sizes[1]):
            ends = [p if k == 0 else partner(p, n, k) for p, n, k in zip((i, j), sizes, kinds, strict=True)]
            if ends[0] is None:
                ends = [i, partner(j, sizes[1], 1)] if fill else None
            elif ends[1] is None:
                ends = [partner(i, sizes[0], 1) if kinds[0] == 0 else ends[0], j] if fill else None
            if ends is not None:
                route.append((i * sizes[1] + j, ends[0] * sizes[1] + ends[1]))
    return lax.ppermute(block, axes, route)


def vmem(n):
    return [pl.BlockSpec(memory_space=pltpu.VMEM)] * n


def vmem(n):
    return [pl.BlockSpec(memory_space=pltpu.VMEM)] * n


def anywhere(n):
    return [pl.BlockSpec(memory_space=pl.ANY)] * n


def body(mode_shapes, stress_field, displacement, material, fixed_nodes, eigenvalues, mode_weight):
    nx, ny, nz = material.shape
    dims = (nx, ny)
    width = nx + 3
    sds = jax.ShapeDtypeStruct
    tile = (MODES, LANES)
    layer = 6 * ny + ny // 2
    zkinds = (1,) if lax.axis_size("gz") == 2 else (1, 2)
    zcount = len(zkinds)
    tiles, x1, x2, edge, ex1, ex2, tables = pl.pallas_call(
        functools.partial(pack_kernel, dims, zcount),
        out_shape=(
            sds((GROUPS, nx, ny) + tile, BF16),
            sds((layer,) + tile, BF16),
            sds((layer,) + tile, BF16),
            sds((GROUPS,) + tile, BF16),
            sds((GROUPS,) + tile, BF16),
            sds((GROUPS,) + tile, BF16),
            sds((3 * zcount * LANES, 2 * LANES), BF16),
        ),
        in_specs=anywhere(4),
        out_specs=tuple(vmem(7)),
        scratch_shapes=[
            pltpu.VMEM(mode_shapes.shape, BF16),
            pltpu.VMEM(material.shape, material.dtype),
            pltpu.VMEM(fixed_nodes.shape, fixed_nodes.dtype),
            pltpu.VMEM(displacement.shape, F32),
            pltpu.VMEM((GROUPS * MODES * PITCH, LANES), F32),
            pltpu.VMEM((ny * LANES, LANES), BF16),
            pltpu.SemaphoreType.DMA((6,)),
        ],
        compiler_params=pltpu.CompilerParams(vmem_limit_bytes=8 << 20),
        name="pack",
    )(*(pltpu.with_memory_space_constraint(a, pltpu.HBM) for a in (mode_shapes, material, fixed_nodes, displacement)))

    xz = ("gx", "gz")
    r2 = swap(x2, xz, (2, 0), True)
    r1 = swap(x1, xz, (1, 0), True)
    rz = [swap(edge, xz, (0, k), True) for k in zkinds]
    rz1 = [swap(ex1, xz, (1, k), True) for k in zkinds]
    rz2 = [swap(ex2, xz, (2, k), True) for k in zkinds]
    count = 6 * width + (nx + 2) // 2 + GROUPS
    y1, y2 = pl.pallas_call(
        functools.partial(merge_kernel, dims, zcount),
        out_shape=(sds((count,) + tile, BF16), sds((count,) + tile, BF16)),
        in_specs=vmem(4 + 3 * zcount),
        out_specs=tuple(vmem(2)),
        scratch_shapes=[pltpu.VMEM((2, nx + 2, HALF, LANES), F32)],
        compiler_params=pltpu.CompilerParams(vmem_limit_bytes=8 << 20),
        name="merge",
    )(*rz2, *rz1, *rz, r2, r1, tiles, tables)

    yz = ("gy", "gz")
    ry1 = swap(y1, yz, (1, 0), True)
    ry2 = swap(y2, ("gx", "gy"), (0, 2), True)
    sens, wmain, field, cell, zr, scale = pl.pallas_call(
        functools.partial(inner_kernel, dims, zcount),
        out_shape=(
            sds((MODES * nx * ny, LANES), F32),
            sds((6, nx + 2, 8, LANES), F32),
            sds((FIELDS, nx + 2, ny, LANES), F32),
            sds((7, nx, ny, LANES), F32),
            sds((GROUPS, width) + tile, F32),
            sds((3,) + tile, F32),
        ),
        in_specs=vmem(4 + 3 * zcount) + [pl.BlockSpec(memory_space=pltpu.SMEM)] * 2,
        out_specs=tuple(vmem(6)),
        scratch_shapes=[
            pltpu.VMEM((GROUPS, width) + tile, F32),
            pltpu.VMEM((3, width, ny) + tile, BF16),
            pltpu.VMEM((ny, 3, width) + tile, F32),
            pltpu.VMEM((ny, 3, width) + tile, F32),
            pltpu.VMEM((nx + 2, 6, ny - 1, 8, LANES), F32),
            pltpu.VMEM(((nx + 2) * ny * HALF, LANES), F32),
            pltpu.VMEM((2 * LANES, 2 * LANES), BF16),
        ],
        compiler_params=pltpu.CompilerParams(vmem_limit_bytes=24 << 20),
        cost_estimate=pl.CostEstimate(flops=20_000_000, bytes_accessed=12_000_000, transcendentals=0),
        name="inner",
    )(*rz, *rz1, *rz2, tiles, r1, r2, stress_field, eigenvalues, mode_weight)
    sens, adjoint = pl.pallas_call(
        functools.partial(final_kernel, dims),
        out_shape=(sds((MODES * nx * ny, LANES), F32), sds((nx, ny, LANES), F32)),
        in_specs=vmem(10),
        out_specs=(pl.BlockSpec(memory_space=pl.ANY), pl.BlockSpec(memory_space=pltpu.VMEM)),
        scratch_shapes=[
            pltpu.VMEM((5, 3 * width) + tile, BF16),
            pltpu.VMEM((2, (nx + 2) // 2) + tile, F32),
            pltpu.VMEM((2, GROUPS) + tile, F32),
            pltpu.VMEM((5, 3, width) + tile, F32),
            pltpu.VMEM((5, 3, width) + tile, F32),
            pltpu.VMEM((6, 3, 8, LANES), F32),
            pltpu.VMEM((6, nx + 2, 16, 2 * LANES), F32),
            pltpu.VMEM((GROUPS, LANES, LANES), F32),
            pltpu.VMEM((FIELDS, nx + 2, 24, LANES), F32),
            pltpu.VMEM((8, 2, 24, LANES), F32),
            pltpu.VMEM((6, nx + 1, 2, 16, LANES), F32),
            pltpu.VMEM((2, 24, LANES), F32),
            pltpu.VMEM((MODES * nx * ny, LANES), F32),
            pltpu.VMEM((2 * LANES, 2 * LANES), BF16),
            pltpu.SemaphoreType.DMA,
        ],
        compiler_params=pltpu.CompilerParams(vmem_limit_bytes=24 << 20),
        name="finish",
    )(y1, y2, ry1, ry2, wmain, field, cell, zr, scale, sens)
    return sens.reshape(MODES, nx, ny, nz), adjoint


def solution(mesh):
    return jax.shard_map(
        body,
        mesh=mesh,
        in_specs=(
            P(None, None, "gx", "gy", "gz"),
            P(None, "gx", "gy", "gz"),
            P(None, "gx", "gy", "gz"),
            P("gx", "gy", "gz"),
            P("gx", "gy", "gz"),
            P(),
            P(),
        ),
        out_specs=(P(None, "gx", "gy", "gz"), P("gx", "gy", "gz")),
        check_vma=False,
    )
```

```python
import functools
import math

import jax
import jax.numpy as jnp
from jax import lax
from jax.experimental import pallas as pl
from jax.experimental.pallas import tpu as pltpu
from jax.sharding import PartitionSpec as P

LEVELS = 8
POISSON = 0.45
LAM = POISSON / ((1.0 + POISSON) * (1.0 - 2.0 * POISSON))
MU = 0.5 / (1.0 + POISSON)
R3 = 1.0 / math.sqrt(3.0)
F32 = jnp.float32
BF16 = jnp.bfloat16
MODES = 16
GROUPS = 4
LANES = 128


def lane_iota(shape=(MODES, LANES)):
    return lax.broadcasted_iota(jnp.int32, shape, len(shape) - 1)


def row_iota(shape):
    return lax.broadcasted_iota(jnp.int32, shape, 0)


def roll(value, shift, axis=1):
    size = value.shape[axis]
    if isinstance(shift, int):
        shift = shift % size
        if shift == 0:
            return value
    return pltpu.roll(value, shift, axis)


def place(axis):
    me = lax.axis_index(axis)
    size = lax.axis_size(axis)
    even = lax.rem(me, 2) == 0
    return even, me > 0, me < size - 1


HALF = 8
PITCH = 33


def pair_up(first, second):
    return jnp.concatenate([first[:HALF].astype(F32), second[:HALF].astype(F32)], 0).astype(BF16)


def pack_kernel(dims, zcount, modes_in, material_in, fixed_in, disp_in, eig_in, weight_in, tiles, x1, x2, edge, ex1, ex2, tables, scale, modes, material, fixed, disp, eig, weight, raw, chosen, sems):
    nx, ny = dims
    copies = [
        pltpu.make_async_copy(src, dst, sems.at[i])
        for i, (src, dst) in enumerate(
            [(modes_in.at[c], modes.at[c]) for c in range(3)]
            + [(material_in, material), (fixed_in, fixed), (disp_in, disp), (eig_in, eig), (weight_in, weight)]
        )
    ]
    for copy in copies:
        copy.start()
    part = nx * ny
    col = lane_iota((LANES, LANES))
    kind = lax.rem(col, 3)
    wanted = jnp.where(row_iota((LANES, LANES)) == jnp.where(kind == 0, LANES - 1, kind - 1), 1.0, 0.0)
    for y in range(ny):
        table = jnp.where((col >= 3 * y) & (col < 3 * y + 3), wanted, 0.0)
        chosen[y * LANES : (y + 1) * LANES, :] = table.astype(BF16)

    def store_table(index, table):
        tables[index * LANES : (index + 1) * LANES, :] = table

    rim_tables(dims, zcount, store_table)

    def store(c, m, value):
        start = (c * MODES + m) * PITCH
        raw[start : start + part, :] = value.reshape(part, LANES)

    def spread(c):
        @pl.loop(0, nx)
        def _(x):
            for y in range(ny):
                value = raw[pl.ds(c * MODES * PITCH + x * ny + y, MODES, stride=PITCH), :]
                tiles[c, x, y] = value.astype(BF16)

    for c in range(3):
        copies[c].wait()
        for m in range(MODES):
            store(c, m, modes[c, m].astype(F32))
        spread(c)
    for copy in copies[3:]:
        copy.wait()
    store(3, 0, material[...].astype(F32) + 1.0)
    store(3, 1, 1.0 - fixed[...].astype(F32))
    for c in range(3):
        value = disp[c]
        first = value.astype(BF16).astype(F32)
        store(3, 2 + c, first)
        store(3, 5 + c, value - first)
    for m in range(HALF, MODES):
        store(3, m, jnp.zeros((part, LANES), F32))

    mode_row = row_iota((MODES, LANES))
    mode_lane = lax.rem(lane_iota(), MODES)
    eig_rows = jnp.zeros((MODES, LANES), F32)
    coef_rows = jnp.zeros((MODES, LANES), F32)
    coef_lanes = jnp.zeros((MODES, LANES), F32)
    for m in range(MODES):
        product = eig[m] * weight[m]
        eig_rows = jnp.where(mode_row == m, eig[m], eig_rows)
        coef_rows = jnp.where(mode_row == m, product, coef_rows)
        coef_lanes = jnp.where(mode_lane == m, product, coef_lanes)
    scale[0], scale[1], scale[2] = eig_rows, coef_rows, coef_lanes
    spread(3)

    block = jnp.concatenate([tiles[:, :, y].reshape(GROUPS * nx * MODES, LANES) for y in range(ny)], 1)
    ends = jnp.dot(block, chosen[...], preferred_element_type=F32)
    ends = ends.reshape(GROUPS, nx, MODES, LANES)
    pieces = LANES // nx
    even, _, _ = place("gx")
    last = [ends[c, nx - 1] for c in range(GROUPS)]
    for c in range(GROUPS):
        total = ends[c, 0]
        for x in range(1, nx):
            total = total + roll(ends[c, x], pieces * x)
        edge[c] = total.astype(BF16)
    for out, out_edge, upward in ((x1, ex1, even), (x2, ex2, jnp.logical_not(even))):
        flag = upward.astype(F32)
        for s in range(2):
            layer = jnp.where(upward, nx - 1, s)
            for c in range(3):
                for y in range(ny):
                    out[(c * 2 + s) * ny + y] = tiles[c, layer, y]
        layer = jnp.where(upward, nx - 1, 0)
        for y in range(0, ny, 2):
            out[6 * ny + y // 2] = pair_up(tiles[3, layer, y], tiles[3, layer, y + 1])
        for c in range(GROUPS):
            below = ends[c, 0] + roll(ends[c, 1], pieces)
            out_edge[c] = (last[c] * flag + below * (1.0 - flag)).astype(BF16)


def pick(parity, lower, upper, first, second, use_lower, use_upper, none_lower, none_upper):
    odd = jnp.logical_not(parity)
    pl.when(jnp.logical_and(lower, parity))(lambda: use_lower(second))
    pl.when(jnp.logical_and(lower, odd))(lambda: use_lower(first))
    pl.when(jnp.logical_and(upper, parity))(lambda: use_upper(first))
    pl.when(jnp.logical_and(upper, odd))(lambda: use_upper(second))
    pl.when(jnp.logical_not(lower))(none_lower)
    pl.when(jnp.logical_not(upper))(none_upper)


def z_partners(zcount):
    even, lower, upper = place("gz")
    lower, upper = lower.astype(F32), upper.astype(F32)
    if zcount == 1:
        return [(lower, upper)]
    even = even.astype(F32)
    return [(lower * (1.0 - even), upper * even), (lower * even, upper * (1.0 - even))]


def z_partners(zcount):
    even, lower, upper = place("gz")
    lower, upper = lower.astype(F32), upper.astype(F32)
    if zcount == 1:
        return [(lower, upper)]
    even = even.astype(F32)
    return [(lower * (1.0 - even), upper * even), (lower * even, upper * (1.0 - even))]


def rim_tables(dims, zcount, store):
    nx, ny = dims
    pieces = LANES // nx
    xe, xlo, xup = place("gx")
    ye, _, _ = place("gy")
    xe, xlo, xup = xe.astype(F32), xlo.astype(F32), xup.astype(F32)
    row = row_iota((LANES, 2 * LANES))
    col = lane_iota((LANES, 2 * LANES))
    second = col >= LANES
    col = lax.rem(col, LANES)
    turn = lax.rem(row, pieces)
    slot = row // pieces
    end = lax.rem(col, 16)
    layer = col // 16
    last = jnp.where(ye, 3 * ny - 3, 0)
    first_row = jnp.where(second, 3 * ny - 3 - last, last)
    fits = (turn == end + first_row) & (turn < 3 * ny) & (end < 6)
    low = lax.rem(turn, 3) == 0
    own = jnp.where(layer == slot + 1, 1.0, 0.0)
    below = jnp.where((layer == 0) & (slot == 0), xlo, 0.0)
    above = jnp.where((layer == slot + nx + 1) & (slot < 2), xup, 0.0)
    by_kind = (below * xe + above * (1.0 - xe), above * xe + below * (1.0 - xe), own)
    for z, (lower, upper) in enumerate(z_partners(zcount)):
        valid = jnp.where(fits, jnp.where(low, lower, upper), 0.0)
        for k, kind in enumerate(by_kind):
            store(k * zcount + z, (valid * kind).astype(BF16))


def cross_xy(a, b):
    return a[0] * b[1] + a[4] * b[5]


def cross_xz(a, b):
    return a[0] * b[2] + a[3] * b[5]


def cross_yz(a, b):
    return a[1] * b[2] + a[3] * b[4]


def squares(a):
    f, g, h, t = a[3] * a[3], a[4] * a[4], a[5] * a[5], a[6] * a[6]
    ft = f + t
    return (a[0] * a[0] + (ft + g), a[1] * a[1] + (ft + h), a[2] * a[2] + ((g + t) + h))


def combos(now, after):
    return (
        now[1] + after[1],
        after[0] - now[0],
        now[2] + after[2],
        (after[1] - now[1]) * R3,
        (now[3] + after[3]) * R3,
        (after[2] - now[2]) * R3,
        (after[3] - now[3]) * (1.0 / 3.0),
    )


def forms(parts, with_energy):
    own = [squares(p) for p in parts]
    quad = [own[0][i] + own[1][i] + own[2][i] for i in range(3)]
    for f in (cross_yz, cross_xz, cross_xy):
        quad.append(f(parts[0], parts[0]) + f(parts[1], parts[1]) + f(parts[2], parts[2]))
    if not with_energy:
        return quad, None
    x, y, z = parts
    energy = (
        MU * (quad[0] + quad[1] + quad[2])
        + (LAM + MU) * (own[0][0] + own[1][1] + own[2][2])
        + (2.0 * LAM) * (cross_xy(x, y) + cross_xz(x, z) + cross_yz(y, z))
        + (2.0 * MU) * (cross_xy(y, x) + cross_xz(z, x) + cross_yz(z, y))
    )
    return quad, energy


def bilinear(l, d):
    total = None
    diagonal = None
    for p in range(3):
        prod = [l[p][i] * d[p][i] for i in range(7)]
        ft = prod[3] + prod[6]
        three = (
            prod[0] + (ft + prod[4]),
            prod[1] + (ft + prod[5]),
            prod[2] + ((prod[4] + prod[6]) + prod[5]),
        )
        whole = three[0] + three[1] + three[2]
        total = whole if total is None else total + whole
        diagonal = three[p] if diagonal is None else diagonal + three[p]
    lx, ly, lz = l
    dx, dy, dz = d
    mixed = (
        (cross_xy(lx, dy) + cross_xy(dx, ly))
        + (cross_xz(lx, dz) + cross_xz(dx, lz))
        + (cross_yz(ly, dz) + cross_yz(dy, lz))
    )
    shear = (
        (cross_xy(dy, lx) + cross_xy(ly, dx))
        + (cross_xz(dz, lx) + cross_xz(lz, dx))
        + (cross_yz(dz, ly) + cross_yz(lz, dy))
    )
    return MU * total + (LAM + MU) * diagonal + LAM * mixed + MU * shear


def fold_rows(values):
    row = row_iota((8, LANES))
    top = row < 4
    step = [
        jnp.where(top, values[k], values[k + 4]) + roll(jnp.where(top, values[k + 4], values[k]), 4, 0)
        for k in range(4)
    ]
    top = lax.rem(row, 4) < 2
    step = [
        jnp.where(top, step[k] + roll(step[k], 6, 0), step[k + 2] + roll(step[k + 2], 2, 0)) for k in range(2)
    ]
    return jnp.where(lax.rem(row, 2) == 0, step[0] + roll(step[0], 7, 0), step[1] + roll(step[1], 1, 0))


def z_table():
    row = row_iota((LANES, 2 * LANES))
    col = lane_iota((LANES, 2 * LANES))
    z = jnp.where(col < LANES, col, col - LANES)
    own = jnp.where(row == z, jnp.where(col < LANES, 1.0, -1.0), 0.0)
    return (own + jnp.where(row == z + 1, 1.0, 0.0)).astype(BF16)


def rim_table(kind):
    row = row_iota((LANES, 2 * LANES))
    z = lax.rem(lane_iota((LANES, 2 * LANES)), LANES)
    return jnp.where((z == LANES - 1) & (row == kind), 1.0, 0.0).astype(BF16)


def first_column(lane_to):
    return jnp.where((row_iota((LANES, LANES)) == 0) & (lane_iota((LANES, LANES)) == lane_to), 1.0, 0.0).astype(BF16)


def rows_along_z(block, rim, kind, table, sz, dz, at):
    table[LANES:, :] = rim_table(kind)
    both = jnp.dot(jnp.concatenate([block, rim], 1), table[...], preferred_element_type=F32)
    sz[at] = both[:, :LANES].reshape(sz.shape[1:])
    dz[at] = both[:, LANES:].reshape(dz.shape[1:])


def x_parts(sz, dz, y, x, h):
    found = []
    for c in range(3):
        s0 = sz[y, c, x, pl.ds(8 * h, 8), :]
        s1 = sz[y, c, x + 1, pl.ds(8 * h, 8), :]
        d0 = dz[y, c, x, pl.ds(8 * h, 8), :]
        d1 = dz[y, c, x + 1, pl.ds(8 * h, 8), :]
        found.append((s0 + s1, s1 - s0, d0 + d1, d1 - d0))
    return found


def mode_value(quad, energy, fields, eig_rows):
    terms = [fields[i] * quad[i] for i in range(6)]
    total = ((terms[0] + terms[1]) + (terms[2] + terms[3])) + (terms[4] + terms[5])
    return fields[6] * energy + eig_rows * total


W_ROWS = 40


def merge_kernel(dims, zcount, *refs):
    nx, ny = dims
    zblocks = refs[: 3 * zcount]
    r2, r1, tiles, tables, scale, y1, y2, rows, rows_aux, ends, sz, dz, part = refs[3 * zcount :]
    xe, xlo, xup = place("gx")
    ye, _, _ = place("gy")
    width = nx + 3
    lane = lane_iota()
    outs = (y1, y2)
    blank = jnp.zeros((MODES, LANES), BF16)
    blank_half = jnp.zeros((HALF, LANES), F32)
    kinds = (0, 1, ny - 1)

    def half_of(ref, row):
        start = row % 2 * HALF
        return ref[6 * ny + row // 2].astype(F32)[start : start + HALF]

    def lower(ref):
        for i, row in enumerate(kinds):
            for c in range(3):
                rows[i, c * width] = ref[c * 2 * ny + row]
            rows_aux[i, 0] = half_of(ref, row)

    def upper(ref):
        for i, row in enumerate(kinds):
            for c in range(3):
                for t in range(2):
                    rows[i, c * width + nx + 1 + t] = ref[(c * 2 + t) * ny + row]
            rows_aux[i, nx + 1] = half_of(ref, row)

    def no_lower():
        for i in range(3):
            for c in range(3):
                rows[i, c * width] = blank
            rows_aux[i, 0] = blank_half

    def no_upper():
        for i in range(3):
            for c in range(3):
                for t in range(2):
                    rows[i, c * width + nx + 1 + t] = blank
            rows_aux[i, nx + 1] = blank_half

    pick(xe, xlo, xup, r1, r2, lower, upper, no_lower, no_upper)
    for i, row in enumerate(kinds):
        for x in range(nx):
            for c in range(3):
                rows[i, c * width + x + 1] = tiles[c, x, row]
            rows_aux[i, x + 1] = tiles[3, x, row][:HALF].astype(F32)

    side = jnp.concatenate([ref[...].reshape(GROUPS * MODES, LANES) for ref in zblocks], 1)
    found = jnp.dot(side, tables[...], preferred_element_type=F32)
    for k in range(2):
        ends[k] = found[:, k * LANES : (k + 1) * LANES].reshape(GROUPS, MODES, LANES)
    down = jnp.where(ye, 1, 0)

    count = 3 * width * MODES
    table = z_table()
    beyond = [ends[down, c] for c in range(3)]
    for i in range(2):
        both = jnp.dot(rows[i].reshape(count, LANES), table, preferred_element_type=F32)
        both = both.reshape(3, width, MODES, 2 * LANES)
        for c in range(3):
            for x in range(width):
                more = roll(beyond[c], LANES - 1 - (16 * x + 3 * i + 1))
                more = jnp.where(lane == LANES - 1, more, 0.0)
                sz[i, c, x] = both[c, x, :, :LANES] + more
                dz[i, c, x] = both[c, x, :, LANES:] + more
    for c in range(3):
        value = beyond[c]
        for x in range(width):
            value = jnp.where(lane == 16 * x + 6, roll(rows[1, c * width + x].astype(F32), 16 * x + 6), value)
        ends[down, c] = value

    values = []
    for x in range(nx + 2):
        for h in range(2):
            coef = scale[1, 8 * h : 8 * h + 8]
            now, after = x_parts(sz, dz, 0, x, h), x_parts(sz, dz, 1, x, h)
            quad, _ = forms([combos(now[c], after[c]) for c in range(3)], False)
            for i in range(6):
                if h == 0:
                    part[x, i] = coef * quad[i]
                else:
                    part[x, i] += coef * quad[i]
        values += [part[x, i] for i in range(6)]
    values += [jnp.zeros((8, LANES), F32)] * (W_ROWS - len(values))
    summed = jnp.concatenate([fold_rows(values[i : i + 8]) for i in range(0, W_ROWS, 8)], 0)
    first = summed.astype(BF16).astype(F32)
    sent = jnp.concatenate([first, summed - first], 0).astype(BF16).reshape(2 * W_ROWS // MODES, MODES, LANES)

    base = 3 * width
    for k, out in enumerate(outs):
        kind = jnp.where(ye, 2 if k == 0 else 0, 0 if k == 0 else 2)
        for i in range(base):
            out[i] = rows[kind, i]
        for x in range(0, nx + 2, 2):
            out[base + x // 2] = pair_up(rows_aux[kind, x], rows_aux[kind, x + 1])
        at = base + (nx + 2) // 2
        out[at : at + GROUPS] = ends[k].astype(BF16)
        out[at + GROUPS :] = sent


FIELDS = 5


def inner_kernel(dims, zcount, *refs):
    rz = refs[:zcount]
    rz1 = refs[zcount : 2 * zcount]
    rz2 = refs[2 * zcount : 3 * zcount]
    tiles, r1, r2, stress, scale = refs[3 * zcount : 3 * zcount + 5]
    sens, wmain, field, cell, zr, rim, full, sz, dz, part, aux, table = refs[3 * zcount + 5 :]
    nx, ny = dims
    width = nx + 3
    tall = ny + 3
    lane = lane_iota()
    xe, xlo, xup = place("gx")
    table[0:LANES, :] = z_table()

    pieces = LANES // nx
    sides = z_partners(zcount)
    low_lane = (lane < 3 * ny) & (lax.rem(lane, 3) == 0)
    high_lane = (lane < 3 * ny) & (lax.rem(lane, 3) != 0)

    def merged(blocks, slot):
        total = None
        for block, (lo, up) in zip(blocks, sides, strict=True):
            mask = jnp.where(low_lane, lo, 0.0) + jnp.where(high_lane, up, 0.0)
            term = roll(block.astype(F32), LANES - pieces * slot) * mask
            total = term if total is None else total + term
        return total

    for c in range(GROUPS):
        for x in range(nx):
            rim[c, x + 1] = merged([r[c] for r in rz], x)

    def rim_lower(refs):
        for c in range(GROUPS):
            rim[c, 0] = merged([r[c] for r in refs], 0)

    def rim_upper(refs):
        for c in range(GROUPS):
            for s in range(2):
                rim[c, nx + 1 + s] = merged([r[c] for r in refs], s)

    def rim_no_lower():
        rim[:, 0] = jnp.zeros((GROUPS, MODES, LANES), F32)

    def rim_no_upper():
        rim[:, nx + 1 : nx + 3] = jnp.zeros((GROUPS, 2, MODES, LANES), F32)

    pick(xe, xlo, xup, rz1, rz2, rim_lower, rim_upper, rim_no_lower, rim_no_upper)

    full[:, 1 : nx + 1] = tiles[0:3]
    for x in range(nx):
        for y in range(ny):
            aux[((x + 1) * ny + y) * HALF : ((x + 1) * ny + y + 1) * HALF, :] = tiles[3, x, y][:HALF].astype(F32)

    def halves(ref, x):
        for i in range(ny // 2):
            start = (x * ny + 2 * i) * HALF
            aux[start : start + 2 * HALF, :] = ref[6 * ny + i].astype(F32)

    def lower(ref):
        for c in range(3):
            for y in range(ny):
                full[c, 0, y] = ref[c * 2 * ny + y]
        halves(ref, 0)

    def upper(ref):
        for c in range(3):
            for s in range(2):
                for y in range(ny):
                    full[c, nx + 1 + s, y] = ref[(c * 2 + s) * ny + y]
        halves(ref, nx + 1)

    def no_lower():
        full[:, 0:1] = jnp.zeros((3, 1, ny, MODES, LANES), BF16)
        aux[0 : ny * HALF, :] = jnp.zeros((ny * HALF, LANES), F32)

    def no_upper():
        full[:, nx + 1 : nx + 3] = jnp.zeros((3, 2, ny, MODES, LANES), BF16)
        aux[(nx + 1) * ny * HALF : (nx + 2) * ny * HALF, :] = jnp.zeros((ny * HALF, LANES), F32)

    pick(xe, xlo, xup, r1, r2, lower, upper, no_lower, no_upper)

    count = 3 * width * MODES
    ends = rim[0:3].reshape(count, LANES).astype(BF16)
    column = None
    for y in range(ny):
        block = full[:, :, y].reshape(count, LANES)
        rows_along_z(block, ends, 3 * y + 1, table, sz, dz, y)
        term = jnp.dot(block, first_column(3 * tall + y + 1), preferred_element_type=F32)
        column = term if column is None else column + term
    column = column.reshape(3, width, MODES, LANES)
    for c in range(GROUPS):
        for x in range(width):
            turned = roll(rim[c, x], 3)
            zr[c, x] = turned + column[c, x] if c < 3 else turned

    for x in range(nx + 2):
        def channel(k):
            return aux[pl.ds(x * ny * HALF + k, ny, stride=HALF), :]

        field[0, x] = channel(0)
        field[1, x] = channel(1)
        for c in range(3):
            field[2 + c, x] = channel(2 + c) + channel(5 + c)

    for x in range(nx):
        density = field[0, x + 1] * (1.0 / LEVELS)
        young = 0.001 + density * density * density
        slope = 3.0 * density * density
        ratio = slope / young
        cell[6, x] = slope * (1.0 / 16.0)
        for c in range(6):
            cell[c, x] = stress[c, x] * ratio * (-1.0 / 16.0 if c < 3 else -1.0 / 8.0)

    def sweep(x, inside):
        for h in range(2):
            coef = scale[1, 8 * h : 8 * h + 8]
            eig_half = scale[0, 8 * h : 8 * h + 8]
            now = x_parts(sz, dz, 0, x, h)
            for y in range(ny - 1):
                after = x_parts(sz, dz, y + 1, x, h)
                quad, energy = forms([combos(now[c], after[c]) for c in range(3)], inside)
                if inside:
                    fields = [cell[i, x - 1, pl.ds(y, 1), :] for i in range(7)]
                    start = 8 * h * nx * ny + (x - 1) * ny + y
                    sens[pl.ds(start, 8, stride=nx * ny), :] = mode_value(quad, energy, fields, eig_half)
                for i in range(6):
                    if h == 0:
                        part[x, i, y] = coef * quad[i]
                    else:
                        part[x, i, y] += coef * quad[i]
                now = after
        blank = jnp.zeros((8, LANES), F32)
        for i in range(6):
            wmain[i, x] = fold_rows([blank] + [part[x, i, y] for y in range(ny - 1)])

    for x in range(1, nx + 1):
        sweep(x, True)
    for x in (0, nx + 1):
        sweep(x, False)


def final_kernel(dims, y1, y2, r1, r2, wmain, field_in, cell, zr, scale, sens_in, sens, adjoint, rows, rows_aux, rows_end, far_w, sz, dz, sum_z, w, zt, field, shear, load, stage, whole, table, sem):
    nx, ny = dims
    width = nx + 3
    tall = ny + 3
    lane = lane_iota()
    ye, ylo, yup = place("gy")
    table[0:LANES, :] = z_table()
    whole[...] = sens_in[...]

    def copy_rows(to, ref):
        for i in range(3 * width):
            rows[to, i] = ref[i]

    aux_base = 3 * width
    end_base = aux_base + (nx + 2) // 2

    def copy_aux(to, ref):
        for i in range((nx + 2) // 2):
            rows_aux[to, i] = ref[aux_base + i].astype(F32)
        for c in range(GROUPS):
            rows_end[to, c] = ref[end_base + c].astype(F32)

    def lower(ref):
        copy_rows(0, ref)
        copy_aux(0, ref)

    def upper(ref):
        copy_rows(3, ref)
        copy_aux(1, ref)
        sent = ref[end_base + GROUPS :].astype(F32).reshape(2 * W_ROWS, LANES)
        far_w[...] = sent[:W_ROWS] + sent[W_ROWS:]

    def no_lower():
        rows[0] = jnp.zeros_like(rows[0])
        rows_aux[0] = jnp.zeros_like(rows_aux[0])
        rows_end[0] = jnp.zeros_like(rows_end[0])

    def no_upper():
        rows[3] = jnp.zeros_like(rows[3])
        rows_aux[1] = jnp.zeros_like(rows_aux[1])
        rows_end[1] = jnp.zeros_like(rows_end[1])
        far_w[...] = jnp.zeros_like(far_w)

    pick(ye, ylo, yup, r1, r2, lower, upper, no_lower, no_upper)

    @pl.when(ye)
    def _():
        copy_rows(2, y1)
        copy_rows(1, y2)

    @pl.when(jnp.logical_not(ye))
    def _():
        copy_rows(2, y2)
        copy_rows(1, y1)

    far = 3 * (ny + 1)
    count = 3 * width * MODES
    at = (0, 1, ny, ny + 1)
    column = None
    for i in (0, 3):
        term = jnp.dot(rows[i].reshape(count, LANES), first_column(3 * tall + at[i]), preferred_element_type=F32)
        column = term if column is None else column + term
    column = column.reshape(3, width, MODES, LANES)
    full_rim = []
    for c in range(GROUPS):
        layers = []
        for x in range(width):
            ends = jnp.where(lane < 3, roll(rows_end[0, c], LANES - 16 * x), zr[c, x])
            ends = jnp.where((lane >= far) & (lane < far + 6), roll(rows_end[1, c], far - 16 * x), ends)
            if c < 3:
                ends = ends + column[c, x]
                corner = 3 * tall + ny + 2
                ends = jnp.where(lane == corner, roll(rows_end[1, c], corner - 6 - 16 * x), ends)
            layers.append(ends)
        layers.append(jnp.zeros((LANES - width * MODES, LANES), F32))
        stacked = jnp.concatenate(layers, 0)
        full_rim.append(stacked[: width * MODES])
        zt[c] = stacked.T
    ends = jnp.concatenate(full_rim[:3], 0).astype(BF16)
    for i in range(4):
        rows_along_z(rows[i].reshape(count, LANES), ends, 3 * at[i] + 1, table, sz, dz, i)

    w[:, :, 0:8, 0:LANES] = wmain[...]
    for x in range(nx + 2):
        for k in range(6):
            w[k, x, ny + 1 : ny + 2, 0:LANES] = far_w[6 * x + k : 6 * x + k + 1, :]

    def sweep(x, inside):
        for h in range(2):
            coef = scale[1, 8 * h : 8 * h + 8]
            for i, (first, own) in enumerate(((0, False), (2, inside))):
                now = x_parts(sz, dz, first, x, h)
                after = x_parts(sz, dz, first + 1, x, h)
                quad, energy = forms([combos(now[c], after[c]) for c in range(3)], own)
                if own:
                    fields = [cell[k, x - 1, ny - 1 : ny, :] for k in range(7)]
                    start = 8 * h * nx * ny + x * ny - 1
                    value = mode_value(quad, energy, fields, scale[0, 8 * h : 8 * h + 8])
                    whole[pl.ds(start, 8, stride=nx * ny), :] = value
                for k in range(6):
                    if h == 0:
                        sum_z[k, i] = coef * quad[k]
                    else:
                        sum_z[k, i] += coef * quad[k]
        pairs = [(k, i) for k in range(6) for i in range(2)]
        for start in range(0, len(pairs), 8):
            some = pairs[start : start + 8]
            values = [sum_z[k, i] for k, i in some]
            values += [jnp.zeros((8, LANES), F32)] * (8 - len(some))
            folded = fold_rows(values)
            for j, (k, i) in enumerate(some):
                row = (0, ny)[i]
                w[k, x, row : row + 1, 0:LANES] = folded[j : j + 1]

    for x in range(1, nx + 1):
        sweep(x, True)
    for x in (0, nx + 1):
        sweep(x, False)

    copy = pltpu.make_async_copy(whole, sens, sem)
    copy.start()

    for x in range(nx + 2):
        for k in range(FIELDS):
            field[k, x, 1 : ny + 1] = field_in[k, x]
        for side, row in ((0, 0), (1, ny + 1)):
            pair = rows_aux[side, x // 2][(x % 2) * HALF : (x % 2 + 1) * HALF]
            field[0, x, row : row + 1] = pair[0:1]
            field[1, x, row : row + 1] = pair[1:2]
            for c in range(3):
                field[2 + c, x, row : row + 1] = pair[2 + c : 3 + c] + pair[5 + c : 6 + c]

    def end_nodes(c, kind, y):
        if kind == 3:
            return zt[c, pl.ds(3 * tall + y, 16), :]
        return zt[c, pl.ds(3 * y + kind, 16, stride=3), :]

    def end_parts(low, high, y):
        found = []
        for c in range(3):
            first, second = end_nodes(c, low, y), end_nodes(c, high, y)
            s, d = first + second, second - first
            s_next, d_next = roll(s, LANES - 16), roll(d, LANES - 16)
            found.append((s + s_next, s_next - s, d + d_next, d_next - d))
        return found

    sides = []
    for low, high in ((0, 3), (1, 2)):
        now, after = end_parts(low, high, 0), end_parts(low, high, 1)
        quad, _ = forms([combos(now[c], after[c]) for c in range(3)], False)
        sides.append([value * scale[2] for value in quad])

    def narrow(first, second, shift):
        kept = lax.rem(lane, 2 * shift) < shift
        return jnp.where(kept, first + roll(first, LANES - shift), second + roll(second, shift))

    step = [narrow(sides[0][i], sides[1][i], 1) for i in range(6)]
    step = [narrow(step[i], step[i + 1], 2) for i in (0, 2, 4)]
    step = [narrow(step[0], step[1], 4), step[2] + roll(step[2], LANES - 4)]
    packed = narrow(step[0], step[1], 8)
    for i in range(6):
        for x in range(nx + 2):
            w[i, x, 0:16, LANES:] = roll(packed, LANES - (16 * x + 2 * i + 1))

    def end_field(channel, x, first, with_low):
        value = roll(zt[3, pl.ds(3 * first + 1, 16, stride=3), :], LANES - (16 * x + channel))
        if not with_low:
            return value
        low = roll(zt[3, pl.ds(3 * first, 16, stride=3), :], LANES - 1 - (16 * x + channel))
        return jnp.where(lane == 0, value, jnp.where(lane == LANES - 1, low, 0.0))

    def z_back(main, end):
        turned, turned_end = roll(main, 1), roll(end, 1)
        return jnp.where(lane == 0, turned_end, turned), jnp.where(lane == 0, turned, turned_end)

    first_rows = None
    for x in range(nx + 2):
        level = (field[0, x, 0:16], end_field(0, x, 0, True))
        scaled = []
        for t in range(2):
            density = level[t] * (1.0 / LEVELS)
            young = 0.001 + density * density * density
            young = jnp.where(level[t] > 0.0, young, 0.0) * (1.0 / 64.0)
            value = [w[i, x, 0:16, LANES * t : LANES * (t + 1)] * young for i in range(6)]
            trace = LAM * (value[0] + value[1] + value[2])
            scaled.append(
                [trace + (2.0 * MU) * value[i] for i in range(3)] + [(2.0 * MU) * value[i] for i in range(3, 6)]
            )
        sums, diffs = [], []
        for i in range(6):
            main, end = scaled[0][i], scaled[1][i]
            back_main, back_end = z_back(main, end)
            sums.append((main + back_main, end + back_end))
            diffs.append((main - back_main, end - back_end))
        xx, yy, zz, yz, xz, xy = range(6)
        order = (sums[xx], sums[xy], diffs[xz], sums[yy], diffs[yz], sums[xz], sums[yz], diffs[zz])
        for slot, source in enumerate(order):
            for t in range(2):
                shear[slot, t, 0:16] = source[t]
        found = []
        for t in range(2):
            low = [shear[slot, t, 0:16] for slot in range(8)]
            high = [shear[slot, t, 1:17] for slot in range(8)]
            plus = [low[k] + high[k] for k in range(8)]
            minus = [high[k] - low[k] for k in range(8)]
            found.append([plus[0], minus[1] + plus[2], plus[1], minus[3] + plus[4], plus[5], minus[6] + plus[7]])
        if x > 0:
            node = x - 1
            for t in range(2):
                free = field[1, x, 1:17] if t == 0 else end_field(1, x, 1, False)
                for p in range(3):
                    value = (found[t][2 * p] - first_rows[t][2 * p]) + (
                        found[t][2 * p + 1] + first_rows[t][2 * p + 1]
                    )
                    load[p, node, t] = value * free
                    if t == 0:
                        shift = field[2 + p, x, 1:17]
                    else:
                        shift = end_field(2 + p, x, 1, False) + end_field(5 + p, x, 1, False)
                    load[3 + p, node, t] = shift
        first_rows = found

    def node_layer(x):
        found = []
        for f in range(6):
            main, end = load[f, x, 0], load[f, x, 1]
            after = jnp.where(lane == LANES - 1, roll(end, LANES - 1), roll(main, LANES - 1))
            s, d = main + after, after - main
            stage[0, 0:16] = s
            stage[1, 0:16] = d
            s_next, d_next = stage[0, 1:9], stage[1, 1:9]
            s, d = s[0:8], d[0:8]
            found.append((s + s_next, s_next - s, d + d_next, d_next - d))
        return found

    def layer_combos(now, after):
        return (
            after[0] - now[0],
            now[1] + after[1],
            now[2] + after[2],
            (after[1] - now[1]) * R3,
            (after[2] - now[2]) * R3,
            (now[3] + after[3]) * R3,
            (after[3] - now[3]) * (1.0 / 3.0),
        )

    now = node_layer(0)
    for x in range(nx):
        after = node_layer(x + 1)
        parts = [layer_combos(now[f], after[f]) for f in range(6)]
        adjoint[x] = cell[6, x] * bilinear(parts[:3], parts[3:])
        now = after
    copy.wait()


def partner(index, size, kind):
    other = index ^ 1 if kind == 1 else ((index + 1) ^ 1) - 1
    return other if 0 <= other < size else None


def swap(block, axes, kinds, fill):
    sizes = [lax.axis_size(a) for a in axes]
    route = []
    for i in range(sizes[0]):
        for j in range(sizes[1]):
            ends = [p if k == 0 else partner(p, n, k) for p, n, k in zip((i, j), sizes, kinds, strict=True)]
            if ends[0] is None:
                ends = [i, partner(j, sizes[1], 1)] if fill else None
            elif ends[1] is None:
                ends = [partner(i, sizes[0], 1) if kinds[0] == 0 else ends[0], j] if fill else None
            if ends is not None:
                route.append((i * sizes[1] + j, ends[0] * sizes[1] + ends[1]))
    return lax.ppermute(block, axes, route)


def vmem(n):
    return [pl.BlockSpec(memory_space=pltpu.VMEM)] * n


def vmem(n):
    return [pl.BlockSpec(memory_space=pltpu.VMEM)] * n


def anywhere(n):
    return [pl.BlockSpec(memory_space=pl.ANY)] * n


def body(mode_shapes, stress_field, displacement, material, fixed_nodes, eigenvalues, mode_weight):
    nx, ny, nz = material.shape
    dims = (nx, ny)
    width = nx + 3
    sds = jax.ShapeDtypeStruct
    tile = (MODES, LANES)
    layer = 6 * ny + ny // 2
    zkinds = (1,) if lax.axis_size("gz") == 2 else (1, 2)
    zcount = len(zkinds)
    tiles, x1, x2, edge, ex1, ex2, tables, scale = pl.pallas_call(
        functools.partial(pack_kernel, dims, zcount),
        out_shape=(
            sds((GROUPS, nx, ny) + tile, BF16),
            sds((layer,) + tile, BF16),
            sds((layer,) + tile, BF16),
            sds((GROUPS,) + tile, BF16),
            sds((GROUPS,) + tile, BF16),
            sds((GROUPS,) + tile, BF16),
            sds((3 * zcount * LANES, 2 * LANES), BF16),
            sds((3,) + tile, F32),
        ),
        in_specs=anywhere(6),
        out_specs=tuple(vmem(8)),
        scratch_shapes=[
            pltpu.VMEM(mode_shapes.shape, BF16),
            pltpu.VMEM(material.shape, material.dtype),
            pltpu.VMEM(fixed_nodes.shape, fixed_nodes.dtype),
            pltpu.VMEM(displacement.shape, F32),
            pltpu.SMEM(eigenvalues.shape, F32),
            pltpu.SMEM(mode_weight.shape, F32),
            pltpu.VMEM((GROUPS * MODES * PITCH, LANES), F32),
            pltpu.VMEM((ny * LANES, LANES), BF16),
            pltpu.SemaphoreType.DMA((8,)),
        ],
        compiler_params=pltpu.CompilerParams(vmem_limit_bytes=8 << 20),
        name="pack",
    )(
        *(
            pltpu.with_memory_space_constraint(a, pltpu.HBM)
            for a in (mode_shapes, material, fixed_nodes, displacement, eigenvalues, mode_weight)
        )
    )

    xz = ("gx", "gz")
    r2 = swap(x2, xz, (2, 0), True)
    r1 = swap(x1, xz, (1, 0), True)
    rz = [swap(edge, xz, (0, k), True) for k in zkinds]
    rz1 = [swap(ex1, xz, (1, k), True) for k in zkinds]
    rz2 = [swap(ex2, xz, (2, k), True) for k in zkinds]
    count = 3 * width + (nx + 2) // 2 + GROUPS + 2 * W_ROWS // MODES
    y1, y2 = pl.pallas_call(
        functools.partial(merge_kernel, dims, zcount),
        out_shape=(sds((count,) + tile, BF16), sds((count,) + tile, BF16)),
        in_specs=vmem(5 + 3 * zcount),
        out_specs=tuple(vmem(2)),
        scratch_shapes=[
            pltpu.VMEM((3, 3 * width) + tile, BF16),
            pltpu.VMEM((3, nx + 2, HALF, LANES), F32),
            pltpu.VMEM((2, GROUPS) + tile, F32),
            pltpu.VMEM((2, 3, width) + tile, F32),
            pltpu.VMEM((2, 3, width) + tile, F32),
            pltpu.VMEM((nx + 2, 6, 8, LANES), F32),
        ],
        compiler_params=pltpu.CompilerParams(vmem_limit_bytes=8 << 20),
        name="merge",
    )(*rz2, *rz1, *rz, r2, r1, tiles, tables, scale)

    yz = ("gy", "gz")
    ry1 = swap(y1, yz, (1, 0), True)
    ry2 = swap(y2, ("gx", "gy"), (0, 2), True)
    sens, wmain, field, cell, zr = pl.pallas_call(
        functools.partial(inner_kernel, dims, zcount),
        out_shape=(
            sds((MODES * nx * ny, LANES), F32),
            sds((6, nx + 2, 8, LANES), F32),
            sds((FIELDS, nx + 2, ny, LANES), F32),
            sds((7, nx, ny, LANES), F32),
            sds((GROUPS, width) + tile, F32),
        ),
        in_specs=vmem(5 + 3 * zcount),
        out_specs=tuple(vmem(5)),
        scratch_shapes=[
            pltpu.VMEM((GROUPS, width) + tile, F32),
            pltpu.VMEM((3, width, ny) + tile, BF16),
            pltpu.VMEM((ny, 3, width) + tile, F32),
            pltpu.VMEM((ny, 3, width) + tile, F32),
            pltpu.VMEM((nx + 2, 6, ny - 1, 8, LANES), F32),
            pltpu.VMEM(((nx + 2) * ny * HALF, LANES), F32),
            pltpu.VMEM((2 * LANES, 2 * LANES), BF16),
        ],
        compiler_params=pltpu.CompilerParams(vmem_limit_bytes=24 << 20),
        cost_estimate=pl.CostEstimate(flops=20_000_000, bytes_accessed=12_000_000, transcendentals=0),
        name="inner",
    )(*rz, *rz1, *rz2, tiles, r1, r2, stress_field, scale)
    sens, adjoint = pl.pallas_call(
        functools.partial(final_kernel, dims),
        out_shape=(sds((MODES * nx * ny, LANES), F32), sds((nx, ny, LANES), F32)),
        in_specs=vmem(10),
        out_specs=(pl.BlockSpec(memory_space=pl.ANY), pl.BlockSpec(memory_space=pltpu.VMEM)),
        scratch_shapes=[
            pltpu.VMEM((4, 3 * width) + tile, BF16),
            pltpu.VMEM((2, (nx + 2) // 2) + tile, F32),
            pltpu.VMEM((2, GROUPS) + tile, F32),
            pltpu.VMEM((W_ROWS, LANES), F32),
            pltpu.VMEM((4, 3, width) + tile, F32),
            pltpu.VMEM((4, 3, width) + tile, F32),
            pltpu.VMEM((6, 2, 8, LANES), F32),
            pltpu.VMEM((6, nx + 2, 16, 2 * LANES), F32),
            pltpu.VMEM((GROUPS, LANES, LANES), F32),
            pltpu.VMEM((FIELDS, nx + 2, 24, LANES), F32),
            pltpu.VMEM((8, 2, 24, LANES), F32),
            pltpu.VMEM((6, nx + 1, 2, 16, LANES), F32),
            pltpu.VMEM((2, 24, LANES), F32),
            pltpu.VMEM((MODES * nx * ny, LANES), F32),
            pltpu.VMEM((2 * LANES, 2 * LANES), BF16),
            pltpu.SemaphoreType.DMA,
        ],
        compiler_params=pltpu.CompilerParams(vmem_limit_bytes=24 << 20),
        name="finish",
    )(y1, y2, ry1, ry2, wmain, field, cell, zr, scale, sens)
    return sens.reshape(MODES, nx, ny, nz), adjoint


def solution(mesh):
    return jax.shard_map(
        body,
        mesh=mesh,
        in_specs=(
            P(None, None, "gx", "gy", "gz"),
            P(None, "gx", "gy", "gz"),
            P(None, "gx", "gy", "gz"),
            P("gx", "gy", "gz"),
            P("gx", "gy", "gz"),
            P(),
            P(),
        ),
        out_specs=(P(None, "gx", "gy", "gz"), P("gx", "gy", "gz")),
        check_vma=False,
    )
```
